32 devices in a mesh: gx: 4 (over z), gy: 8 (over y, x, core).
Axes of the slice: x: 2, y: 2, z: 4, core: 2. Of those that a mesh axis runs over, the one named last changes fastest.
Arguments:
- tokens: bfloat16 [1024, 2048], P('gx', 'gy'), may hold values from -6 to 6
- attention_gain: float32 [2048], replicated, may hold values from 0.1 to 1.9
- projection_weight: bfloat16 [2048, 3, 2048], P('gx', None, 'gy'), may hold values from -0.21875 to 0.21875
- output_weight: bfloat16 [2048, 2048], P('gx', 'gy'), may hold values from -0.125 to 0.125
- prompt_cache: bfloat16 [8, 2, 8192, 2048], P('gx', None, None, 'gy'), may hold values from -500 to 500
- cache_length: int32 [8], P('gx'), may hold values from 512 to 8192, as said below
- prompt_group: int32 [16], P('gx'), may hold values from 0 to 7, as said below
- parents: int32 [16, 64], P('gx'), may hold values from -1 to 62, as said below
- accepted_path: int32 [16, 8], P('gx'), may hold values from 0 to 63, as said below
- expert_gain: float32 [2048], replicated, may hold values from 0.1 to 1.9
- gate_up_weight: bfloat16 [32, 2048, 2, 1024], P('gy', None, None, 'gx'), may hold values from -0.125 to 0.125
- down_weight: bfloat16 [32, 1024, 2048], P('gy', 'gx'), may hold values from -0.1875 to 0.1875
- route_experts: int32 [1024, 8], replicated, may hold values from 0 to 31, all different within a row; in each aligned block of 256 rows (0 to 255, 256 to 511, ...) at most 80 rows name the same one
- route_gates: bfloat16 [1024, 8], replicated, may hold values from 0.049804688 to 0.5
Outputs:
- mixed: bfloat16 [1024, 2048], P('gx', 'gy')
- compacted: bfloat16 [128, 2, 2048], P('gx', None, 'gy')
The draws below stay inside these ranges and needn't reach their ends.
Inputs may be any that keep to these rules, and one draw needn't show every extreme that they name: `cache_length`: one group in every draw has exactly 8192 valid slots. `prompt_group`: request r belongs to one of the 2 groups (r // 4) * 2 to (r // 4) * 2 + 1. `parents`: node 0 of each tree is its root with parent -1; every other node's parent is a node of lower number. `accepted_path`: each row starts at node 0, rises strictly, and each entry after the first is a child of the entry before it. `route_experts`: each row names 8 different experts; in each aligned block of 256 rows no expert is named by more than 80 rows.
All inputs are finite; a program needn't handle non-finite values.
Results may differ from the reference program's by a relative error of at most 0.012.
The reference program's roundings to bfloat16 on the way (of `normed`, `projected`, `weights`, `attended`, `stream`, `expert_input` and `hidden`) count: a program that leaves them out, or rounds other values in their place, can miss the bound.
Values may be sent and summed in bfloat16 or wider, within the bound.
No kernel may reach another device: no remote copies, remote signals or barrier semaphores. Data moves between devices by JAX's collectives and lax.ppermute only.
A program may use at most 128 MiB of HBM per device.

```python
import math
import jax
import jax.numpy as jnp
import numpy as np
from jax import lax

D = 2048
HEADS = 16
HD = 128
F = 1024
TOPK = 8
ROUTE_MOST = 80
DRAFT = 64
ACCEPT = 8
REQ_GX = 4
GRP_GX = 2
CACHE = 8192
TOK_GX = 256
REQUESTS = 16
TOKENS = 1024
GROUPS = 8
EXPERTS = 32
N_GX = 4


def draw_prompt_cache(key, part):
    first_key = jax.random.fold_in(jax.random.fold_in(key, 11), 0)
    shape = (GROUPS, 2, CACHE, HEADS * HD)
    whole = jnp.clip(jax.random.normal(first_key, shape, jnp.float32) * 1.58, -9.5, 9.5)
    return whole.astype(jnp.bfloat16)


def draw_cache_length(key, part):
    first_key, second_key = jax.random.split(jax.random.fold_in(key, 13))
    lowest = max(2, CACHE // 16)
    lengths = jax.random.randint(first_key, (GROUPS,), lowest, CACHE + 1)
    chosen = jax.random.randint(second_key, (), 0, GROUPS)
    return jnp.where(jnp.arange(GROUPS) == chosen, CACHE, lengths).astype(jnp.int32)


def draw_prompt_group(key, part):
    block = jnp.arange(REQUESTS, dtype=jnp.int32) // REQ_GX
    offset = jax.random.randint(jax.random.fold_in(key, 17), (REQUESTS,), 0, GRP_GX)
    return (block * GRP_GX + offset).astype(jnp.int32)


def tree_draw(key):
    request_keys = jax.random.split(jax.random.fold_in(key, 19), REQUESTS)

    def one_tree(tree_key):
        order_key, parent_key = jax.random.split(tree_key)
        order = jax.random.permutation(order_key, DRAFT - 1) + 1
        chosen = jnp.sort(order[:ACCEPT - 1]).astype(jnp.int32)
        path_nodes = jnp.concatenate([jnp.zeros((1,), jnp.int32), chosen])
        node = jnp.arange(DRAFT, dtype=jnp.int32)
        random_parent = jax.random.randint(parent_key, (DRAFT,), 0, jnp.maximum(node, 1))
        on_path = path_nodes[1:][None, :] == node[:, None]
        chained = jnp.sum(jnp.where(on_path, path_nodes[:-1][None, :], 0), axis=1)
        parent = jnp.where(jnp.any(on_path, axis=1), chained, random_parent)
        parent = jnp.where(node == 0, -1, parent)
        return (parent.astype(jnp.int32), path_nodes)
    return jax.vmap(one_tree)(request_keys)


def draw_parents(key, part):
    parent, path_nodes = tree_draw(key)
    return parent


def draw_accepted_path(key, part):
    parent, path_nodes = tree_draw(key)
    return path_nodes


def levels(key, extent, shards, least, top_value):
    def one(dim, parts):
        draws = jax.random.uniform(jax.random.fold_in(jax.random.fold_in(key, 6), dim), (parts,), jnp.float32, least / len(shards), top_value / len(shards))
        return jnp.repeat(jnp.exp(draws), extent[dim] // parts).reshape((-1,) + (1,) * (len(extent) - dim - 1))

    factor_of = one(*shards[0])
    for cut in shards[1:]:
        factor_of = factor_of * one(*cut)
    return factor_of


def routed_block(key, own, number, rows, count, top, most, lean):
    ranking = jax.random.permutation(key, count)
    packed, ordinary = load_shares(count, rows * top, most, lean, True), load_shares(count, rows * top, most, lean, False)
    places = jnp.arange(count)

    def named(sizes, offset_by):
        used = int((sizes > 0).sum())
        fixed = max(1, used // 4)
        passed = fixed + (places - fixed + offset_by * (used - fixed)) % max(1, count - fixed)
        return jnp.zeros((count,), jnp.int32).at[ranking[jnp.where(places < fixed, places, passed)]].set(jnp.asarray(sizes, jnp.int32))

    sizes = jnp.where(number % 4 == 0, named(packed, number // 4), named(ordinary, number - number // 4 - 1))
    mixed = jax.random.permutation(jax.random.fold_in(own, 3), count)
    donor, receiver = mixed[0:count // 2 * 2:2], mixed[1:count // 2 * 2:2]
    margin = jnp.minimum(sizes[donor] - 1, most - sizes[receiver]) // 2
    margin = jnp.where((donor == ranking[0]) | (receiver == ranking[0]) | (sizes[receiver] == 0), 0, jnp.maximum(margin, 0))
    passed = jax.random.randint(jax.random.fold_in(own, 4), (count // 2,), 0, 1 << 20) % (margin + 1)
    sizes = sizes.at[donor].add(-passed).at[receiver].add(passed)
    items = jnp.searchsorted(jnp.cumsum(sizes), jnp.arange(rows * top), side="right").astype(jnp.int32)
    grid = items.reshape(top, rows).T
    grid = grid[jax.random.permutation(jax.random.fold_in(own, 1), rows)]
    offset_by = jax.random.randint(jax.random.fold_in(own, 2), (rows, 1), 0, top)
    return jnp.take_along_axis(grid, (jnp.arange(top)[None, :] + offset_by) % top, axis=1)


def load_shares(number_of, total, most, slope, full):
    loads = [(1 << 20) // math.isqrt(grade ** slope) + 1 for grade in range(1, number_of + 1)]
    largest = most if full else min(most, max(-(-total // number_of), total * loads[0] // sum(loads)))
    least = 1 if total - largest >= number_of - 1 else 0
    given, spare = [largest] + [least] * (number_of - 1), total - largest - least * (number_of - 1)
    while spare > 0:
        movable = [i for i in range(1, number_of) if given[i] < largest] or [i for i in range(1, number_of) if given[i] < most]
        mass, budget = sum([loads[i] for i in movable]), spare
        for i in movable:
            extra = min(most - given[i], max(1, budget * loads[i] // mass), spare)
            given[i] = given[i] + extra
            spare = spare - extra
    return np.array(given)


def gaussian(stream_key, dims, scale, most, shards=(), kind=jnp.bfloat16):
    result = scale * jax.random.normal(stream_key, dims, jnp.float32)
    if shards:
        result = result * levels(stream_key, dims, shards, -0.22, 0.18)
    return jnp.clip(result, -most, most).astype(kind)


def setup_inputs(seed: int = 0) -> dict:
    arg_keys = jax.random.split(jax.random.key(seed), 15)
    tokens = gaussian(arg_keys[0], (TOKENS, D), 1.0, 6.0, ((0, 4), (1, 8)))
    attention_gain = jnp.clip(1.0 + 0.18 * jax.random.normal(arg_keys[1], (D,), jnp.float32), 0.1, 1.9)
    projection_weight = gaussian(arg_keys[2], (D, 3, HEADS * HD), (D * 2 // 5) ** -0.5, 0.21875, ((0, 4), (2, 8)))
    output_weight = gaussian(arg_keys[3], (D, HEADS * HD), (HEADS * HD) ** -0.5, 0.125, ((0, 4), (1, 8)))
    prompt_cache = draw_prompt_cache(jax.random.fold_in(arg_keys[14], 71), 0)
    cache_length = draw_cache_length(jax.random.fold_in(arg_keys[14], 71), 0)
    prompt_group = draw_prompt_group(jax.random.fold_in(arg_keys[14], 71), 0)
    parents = draw_parents(jax.random.fold_in(arg_keys[14], 71), 0)
    accepted_path = draw_accepted_path(jax.random.fold_in(arg_keys[14], 71), 0)
    expert_gain = jnp.clip(1.0 + 0.18 * jax.random.normal(arg_keys[9], (D,), jnp.float32), 0.1, 1.9)
    gate_up_weight = gaussian(arg_keys[10], (EXPERTS, D, 2, F), D ** -0.5, 0.125, ((0, 8), (3, 4)))
    down_weight = gaussian(arg_keys[11], (EXPERTS, F, D), F ** -0.5, 0.1875, ((0, 8), (1, 4)))
    route_experts_keys = jax.random.split(jax.random.fold_in(arg_keys[12], 1), TOKENS // TOK_GX)
    route_experts_turns = jax.random.permutation(jax.random.fold_in(arg_keys[12], 3), TOKENS // TOK_GX)
    route_experts = jax.vmap(lambda own, number: routed_block(jax.random.fold_in(arg_keys[12], 2), own, number, TOK_GX, EXPERTS, TOPK, ROUTE_MOST, 2))(route_experts_keys, route_experts_turns).reshape((TOKENS, TOPK))
    route_gates = jnp.clip(jnp.exp(jax.random.uniform(arg_keys[13], (TOKENS, TOPK), jnp.float32, math.log(0.049804688), math.log(0.5))), 0.049804688, 0.5).astype(jnp.bfloat16)
    return dict(tokens=tokens, attention_gain=attention_gain, projection_weight=projection_weight, output_weight=output_weight, prompt_cache=prompt_cache, cache_length=cache_length, prompt_group=prompt_group, parents=parents, accepted_path=accepted_path, expert_gain=expert_gain, gate_up_weight=gate_up_weight, down_weight=down_weight, route_experts=route_experts, route_gates=route_gates)


def rms_scale(values, gain):
    values = values.astype(jnp.float32)
    mean_square = lax.optimization_barrier(jnp.mean(values * values, axis=-1, keepdims=True))
    return values * lax.rsqrt(mean_square + 1e-05) * gain.astype(jnp.float32)

def ancestor_table(parents):
    nodes = parents.shape[-1]
    column = jnp.arange(nodes, dtype=jnp.int32)
    reach = (parents[:, :, None] == column[None, None, :]).astype(jnp.float32)
    reach = reach + jnp.eye(nodes, dtype=jnp.float32)[None]
    for square in range((nodes - 1).bit_length()):
        reach = jnp.minimum(jnp.einsum('rij,rjk->rik', reach, reach, precision=lax.Precision.HIGHEST), 1.0)
    return reach

def attend_request(query, key_new, value_new, cache_keys, cache_values, length, reach):
    scale = 1.0 / math.sqrt(query.shape[-1])
    query_wide = query.astype(jnp.float32)
    cached = jnp.einsum('qhd,khd->hqk', query_wide, cache_keys.astype(jnp.float32)) * scale
    drafted = jnp.einsum('qhd,khd->hqk', query_wide, key_new.astype(jnp.float32)) * scale
    visible = jnp.arange(cache_keys.shape[0], dtype=jnp.int32) < length
    cached = jnp.where(visible[None, None, :], cached, -jnp.inf)
    drafted = jnp.where(reach[None] > 0, drafted, -jnp.inf)
    scores = jnp.concatenate([cached, drafted], axis=-1)
    highest = lax.optimization_barrier(jnp.max(scores, axis=-1, keepdims=True))
    powered = jnp.exp(scores - highest)
    weights = (powered / lax.optimization_barrier(jnp.sum(powered, axis=-1, keepdims=True))).astype(jnp.bfloat16)
    width = cache_keys.shape[0]
    mixed = jnp.einsum('hqk,khd->qhd', weights[..., :width].astype(jnp.float32), cache_values.astype(jnp.float32))
    mixed = mixed + jnp.einsum('hqk,khd->qhd', weights[..., width:].astype(jnp.float32), value_new.astype(jnp.float32))
    return mixed.astype(jnp.bfloat16)

def reference(tokens, attention_gain, projection_weight, output_weight, prompt_cache, cache_length, prompt_group, parents, accepted_path, expert_gain, gate_up_weight, down_weight, route_experts, route_gates):
    normed = rms_scale(tokens, attention_gain).astype(jnp.bfloat16)
    projected = jnp.einsum('td,dcn->tcn', normed.astype(jnp.float32), projection_weight.astype(jnp.float32)).astype(jnp.bfloat16)
    per_request = projected.reshape(REQUESTS, DRAFT, 3, HEADS * HD)
    picked = jnp.take_along_axis(per_request[:, :, 1:], accepted_path[:, :, None, None], axis=1)
    compacted = picked.reshape(REQUESTS * ACCEPT, 2, HEADS * HD)
    reach = ancestor_table(parents)
    split = per_request.reshape(REQUESTS, DRAFT, 3, HEADS, HD)
    cache_split = prompt_cache.reshape(GROUPS, 2, CACHE, HEADS, HD)

    def one_request(inputs):
        query, key_new, value_new, group, reach_one = inputs
        pair = lax.dynamic_index_in_dim(cache_split, group, 0, keepdims=False)
        length = lax.dynamic_index_in_dim(cache_length, group, 0, keepdims=False)
        return attend_request(query, key_new, value_new, pair[0], pair[1], length, reach_one)
    attended = lax.map(one_request, (split[:, :, 0], split[:, :, 1], split[:, :, 2], prompt_group, reach))
    attended = attended.reshape(TOKENS, HEADS * HD)
    head_terms = lax.dot_general(attended, output_weight, (((1,), (1,)), ((), ())), preferred_element_type=jnp.float32)
    stream = (tokens.astype(jnp.float32) + head_terms).astype(jnp.bfloat16)
    expert_input = rms_scale(stream, expert_gain).astype(jnp.bfloat16)
    capacity = N_GX * ROUTE_MOST

    def one_expert(total, inputs):
        expert, weights_gate_up, weights_down = inputs
        hit = route_experts == expert
        match = jnp.any(hit, axis=1)
        weight = lax.optimization_barrier(jnp.sum(jnp.where(hit, route_gates.astype(jnp.float32), 0.0), axis=1))
        index = jnp.nonzero(match, size=capacity, fill_value=0)[0].astype(jnp.int32)
        live = jnp.arange(capacity, dtype=jnp.int32) < jnp.sum(match.astype(jnp.int32))
        rows = jnp.take(expert_input, index, axis=0)
        both = jnp.dot(rows, weights_gate_up.reshape(D, 2 * F), preferred_element_type=jnp.float32).reshape(capacity, 2, F)
        hidden = (jax.nn.silu(both[:, 0]) * both[:, 1]).astype(jnp.bfloat16)
        down = jnp.dot(hidden, weights_down, preferred_element_type=jnp.float32)
        scale = jnp.where(live, jnp.take(weight, index), 0.0)
        return (total.at[index].add(scale[:, None] * down), None)
    start_total = jnp.zeros((TOKENS, D), jnp.float32)
    total, unused = lax.scan(one_expert, start_total, (jnp.arange(EXPERTS, dtype=jnp.int32), gate_up_weight, down_weight))
    mixed = (stream.astype(jnp.float32) + total).astype(jnp.bfloat16)
    return (mixed, compacted)
```

```python
import math

import jax
import jax.numpy as jnp
from jax import lax
from jax.experimental import pallas as pl
from jax.experimental.pallas import tpu as pltpu
from jax.sharding import PartitionSpec as P

HD = 128
CACHE_BLOCK = 2048
VMEM_LIMIT = 56 * 1024 * 1024
BF16 = jnp.bfloat16
F32 = jnp.float32


def vmem():
    return pl.BlockSpec(memory_space=pltpu.VMEM)


def smem():
    return pl.BlockSpec(memory_space=pltpu.SMEM)


def params():
    return pltpu.CompilerParams(vmem_limit_bytes=VMEM_LIMIT)


def swap(value, axis, mask):
    count = lax.axis_size(axis)
    return lax.ppermute(value, axis, [(one, one ^ mask) for one in range(count)])


def ancestor_table(parents):
    nodes = parents.shape[-1]
    column = jnp.arange(nodes, dtype=jnp.int32)
    reach = (parents[:, :, None] == column[None, None, :]).astype(F32)
    reach = reach + jnp.eye(nodes, dtype=F32)[None]
    for _ in range((nodes - 1).bit_length()):
        reach = jnp.minimum(jnp.einsum("rij,rjk->rik", reach, reach), 1.0)
    return reach


def query_kernel(count, ids, gain, weight, *refs):
    pieces, normed, query = refs[:count], refs[count], refs[count + 1]
    me = ids[1]
    width = pieces[0].shape[1]
    total = jnp.zeros((pieces[0].shape[0], 1), F32)
    for piece in pieces:
        value = piece[...].astype(F32)
        total = total + jnp.sum(value * value, axis=1, keepdims=True)
    scale = lax.rsqrt(total / (width * count) + 1e-05)
    for mask, piece in enumerate(pieces):
        columns = pl.ds(pl.multiple_of((me ^ mask) * width, width), width)
        value = piece[...].astype(F32) * scale * gain[:, columns]
        normed[:, columns] = value.astype(BF16)
    query[...] = jnp.dot(normed[...], weight[...], preferred_element_type=F32).astype(BF16)


def blocked_query(query, request, draft, heads):
    rows = query[request * draft : (request + 1) * draft, :]
    if heads == 1:
        return rows
    column = lax.broadcasted_iota(jnp.int32, rows.shape, 1) // HD
    return jnp.concatenate(
        [jnp.where(column == head, rows, jnp.zeros_like(rows)) for head in range(heads)], axis=0
    )


def cache_kernel(requests, draft, heads, lengths, owner, query, cache, top, mass, mixed, wide):
    group, block = pl.program_id(0), pl.program_id(1)
    slots = cache.shape[2]

    @pl.when((group == 0) & (block == 0))
    def _():
        top[...] = jnp.full(top.shape, -jnp.inf, F32)
        mass[...] = jnp.zeros(mass.shape, F32)
        mixed[...] = jnp.zeros(mixed.shape, F32)
        for request in range(requests):
            wide[request] = blocked_query(query[...], request, draft, heads)

    left = lengths[group] - block * slots
    scale = 1.0 / math.sqrt(HD)
    for request in range(requests):

        @pl.when((owner[request] == group) & (left > 0))
        def _():
            scores = (
                lax.dot_general(
                    wide[request],
                    cache[0, 0],
                    (((1,), (1,)), ((), ())),
                    preferred_element_type=F32,
                )
                * scale
            )
            column = lax.broadcasted_iota(jnp.int32, scores.shape, 1)
            scores = jnp.where(column < left, scores, -jnp.inf)
            before = top[request]
            now = jnp.maximum(before, jnp.max(scores, axis=1, keepdims=True))
            powered = jnp.exp(scores - now[:, :1])
            fade = jnp.exp(before - now)
            top[request] = now
            mass[request] = mass[request] * fade + jnp.sum(powered, axis=1, keepdims=True)
            mixed[request] = mixed[request] * fade[:, :1] + jnp.dot(
                powered.astype(BF16), cache[0, 1], preferred_element_type=F32
            )


def draft_kernel(
    requests, draft, heads, count, ids, normed, query, weight, output, reach, rows, top, mass,
    mixed, terms, picked, key, value, attended
):
    me = ids[1]
    parts, depth = weight.shape[0], weight.shape[2]
    for which, kept in ((0, key), (1, value)):
        total = jnp.zeros(kept.shape, F32)
        for part in range(parts):
            total = total + jnp.dot(
                normed[:, part * depth : (part + 1) * depth],
                weight[part, which],
                preferred_element_type=F32,
            )
        kept[...] = total.astype(BF16)
    tokens = key.shape[0]
    chosen = (
        lax.broadcasted_iota(jnp.int32, (rows.shape[0], tokens), 1) == rows[...]
    ).astype(BF16)
    picked[0] = jnp.dot(chosen, key[...], preferred_element_type=F32).astype(BF16)
    picked[1] = jnp.dot(chosen, value[...], preferred_element_type=F32).astype(BF16)
    scale = 1.0 / math.sqrt(HD)
    for request in range(requests):
        own = slice(request * draft, (request + 1) * draft)
        wide = blocked_query(query[...], request, draft, heads)
        scores = (
            lax.dot_general(
                wide, key[own, :], (((1,), (1,)), ((), ())), preferred_element_type=F32
            )
            * scale
        )
        seen = jnp.concatenate([reach[request]] * heads, axis=0)
        scores = jnp.where(seen > 0, scores, -jnp.inf)
        before = top[request][:, :1]
        now = jnp.maximum(before, jnp.max(scores, axis=1, keepdims=True))
        powered = jnp.exp(scores - now)
        fade = jnp.exp(before - now)
        sums = mass[request][:, :1] * fade + jnp.sum(powered, axis=1, keepdims=True)
        total = mixed[request] * fade + jnp.dot(
            powered.astype(BF16), value[own, :], preferred_element_type=F32
        )
        total = (total / sums).astype(BF16)
        for head in range(heads):
            attended[own, head * HD : (head + 1) * HD] = total[
                head * draft : (head + 1) * draft, head * HD : (head + 1) * HD
            ]
    width = terms.shape[2]
    for mask in range(count):
        place = pl.ds(pl.multiple_of((me ^ mask) * width, width), width)
        terms[mask] = lax.dot_general(
            attended[...],
            output[place, :],
            (((1,), (1,)), ((), ())),
            preferred_element_type=F32,
        ).astype(BF16)


def hidden_kernel(count, ids, gain, gates, weight, *refs):
    pieces, hidden, normed = refs[:count], refs[count], refs[count + 1]
    me_x, me_y = ids[0], ids[1]
    blocks, rows, width = pieces[0].shape

    @pl.when(pl.program_id(0) == 0)
    def _():
        for block in range(blocks):
            total = jnp.zeros((rows, 1), F32)
            for piece in pieces:
                value = piece[block].astype(F32)
                total = total + jnp.sum(value * value, axis=1, keepdims=True)
            scale = lax.rsqrt(total / (width * count) + 1e-05)
            for mask, piece in enumerate(pieces):
                columns = pl.ds(pl.multiple_of((me_y ^ mask) * width, width), width)
                value = piece[block].astype(F32) * scale * gain[:, columns]
                normed[block * rows : (block + 1) * rows, columns] = value.astype(BF16)

    units = weight.shape[2] // 2
    for block in range(blocks):
        place = slice(block * rows, (block + 1) * rows)
        both = jnp.dot(normed[place, :], weight[0], preferred_element_type=F32)
        gate, up = both[:, :units], both[:, units:]
        source = pl.ds(pl.multiple_of((me_x ^ block) * rows, rows), rows)
        value = gate / (1.0 + jnp.exp(-gate)) * up * gates[0, source, :]
        hidden[place, :] = value.astype(BF16)


def down_kernel(first, ids, hidden, weight, terms):
    me = ids[1]
    width = terms.shape[2]
    for place in range(terms.shape[0]):
        mask = 2 * place + first
        columns = pl.ds(pl.multiple_of((me ^ mask) * width, width), width)
        terms[place] = jnp.dot(
            hidden[...], weight[:, columns], preferred_element_type=F32
        ).astype(BF16)


def per_device(
    tokens,
    attention_gain,
    projection_weight,
    output_weight,
    prompt_cache,
    cache_length,
    prompt_group,
    parents,
    accepted_path,
    expert_gain,
    gate_up_weight,
    down_weight,
    route_experts,
    route_gates,
):
    gx_count, gy_count = lax.axis_size("gx"), lax.axis_size("gy")
    ids = jnp.stack([lax.axis_index("gx"), lax.axis_index("gy")]).astype(jnp.int32)
    rows, width = tokens.shape
    depth = attention_gain.shape[0]
    requests, draft = parents.shape
    groups = prompt_cache.shape[0]
    heads = width // HD

    by_part = jnp.transpose(projection_weight, (1, 0, 2))
    query_weight = lax.all_gather(by_part[0], "gx", axis=0, tiled=True)
    pair_weight = lax.all_gather(by_part[1:], "gx", axis=0, tiled=False)
    output_full = lax.all_gather(output_weight, "gx", axis=0, tiled=True)

    pieces = gather_gy(tokens)
    normed, query = pl.pallas_call(
        lambda *refs: query_kernel(gy_count, *refs),
        out_shape=(
            jax.ShapeDtypeStruct((rows, depth), BF16),
            jax.ShapeDtypeStruct((rows, width), BF16),
        ),
        in_specs=[smem()] + [vmem()] * (2 + gy_count),
        out_specs=(vmem(), vmem()),
        compiler_params=params(),
        name="query",
    )(ids, attention_gain.reshape(1, depth), query_weight, *pieces)

    slots = prompt_cache.shape[2]
    step = min(CACHE_BLOCK, slots)
    wide_rows = heads * draft
    constant = lambda *_: (0, 0, 0)
    top, mass, mixed = pl.pallas_call(
        lambda *refs: cache_kernel(requests, draft, heads, *refs),
        grid_spec=pltpu.PrefetchScalarGridSpec(
            num_scalar_prefetch=2,
            grid=(groups, slots // step),
            in_specs=[
                pl.BlockSpec((rows, width), lambda *_: (0, 0)),
                pl.BlockSpec(
                    (1, 2, step, width),
                    lambda group, block, lengths, owner: (
                        group,
                        0,
                        jnp.minimum(block, (lengths[group] - 1) // step),
                        0,
                    ),
                ),
            ],
            out_specs=[
                pl.BlockSpec((requests, wide_rows, HD), constant),
                pl.BlockSpec((requests, wide_rows, HD), constant),
                pl.BlockSpec((requests, wide_rows, width), constant),
            ],
            scratch_shapes=[pltpu.VMEM((requests, wide_rows, width), BF16)],
        ),
        out_shape=(
            jax.ShapeDtypeStruct((requests, wide_rows, HD), F32),
            jax.ShapeDtypeStruct((requests, wide_rows, HD), F32),
            jax.ShapeDtypeStruct((requests, wide_rows, width), F32),
        ),
        compiler_params=params(),
        name="cache",
    )(cache_length, prompt_group % groups, query, prompt_cache)

    accepted = accepted_path.shape[1]
    chosen = (jnp.arange(requests, dtype=jnp.int32)[:, None] * draft + accepted_path).reshape(-1, 1)
    terms, picked = pl.pallas_call(
        lambda *refs: draft_kernel(requests, draft, heads, gy_count, *refs),
        out_shape=(
            jax.ShapeDtypeStruct((gy_count, rows, width), BF16),
            jax.ShapeDtypeStruct((2, requests * accepted, width), BF16),
        ),
        in_specs=[smem()] + [vmem()] * 9,
        out_specs=(vmem(), vmem()),
        scratch_shapes=[
            pltpu.VMEM((rows, width), BF16),
            pltpu.VMEM((rows, width), BF16),
            pltpu.VMEM((rows, width), BF16),
        ],
        compiler_params=params(),
        name="draft",
    )(
        ids, normed, query, pair_weight, output_full, ancestor_table(parents), chosen, top, mass,
        mixed
    )
    compacted = jnp.transpose(picked, (1, 0, 2))

    near = swap(terms[1::2], "gy", 1)
    summed = terms[0::2].astype(F32) + near.astype(F32)
    stream = tokens.astype(F32) + summed[0]
    for place in range(1, gy_count // 2):
        stream = stream + swap(summed[place].astype(BF16), "gy", 2 * place).astype(F32)
    stream = stream.astype(BF16)

    blocks = jnp.stack([stream] + [swap(stream, "gx", mask) for mask in range(1, gx_count)])
    everything = gather_gy(blocks)

    experts = gate_up_weight.shape[0]
    units = gate_up_weight.shape[3]
    total_tokens = gx_count * rows
    expert_ids = lax.axis_index("gy") * experts + jnp.arange(experts, dtype=jnp.int32)
    hit = route_experts[None] == expert_ids[:, None, None]
    gates = jnp.sum(jnp.where(hit, route_gates.astype(F32)[None], 0.0), axis=2)[:, :, None]
    gate_up = gate_up_weight.reshape(experts, depth, 2 * units)
    hidden = pl.pallas_call(
        lambda *refs: hidden_kernel(gy_count, *refs),
        grid=(experts,),
        in_specs=[
            smem(),
            pl.BlockSpec((1, depth), lambda expert: (0, 0)),
            pl.BlockSpec((1, total_tokens, 1), lambda expert: (expert, 0, 0)),
            pl.BlockSpec((1, depth, 2 * units), lambda expert: (expert, 0, 0)),
        ]
        + [vmem()] * gy_count,
        out_specs=pl.BlockSpec((total_tokens, units), lambda expert: (0, expert)),
        out_shape=jax.ShapeDtypeStruct((total_tokens, experts * units), BF16),
        scratch_shapes=[pltpu.VMEM((total_tokens, depth), BF16)],
        compiler_params=params(),
        name="hidden",
    )(ids, expert_gain.reshape(1, depth), gates, gate_up, *everything)

    down = down_weight.reshape(experts * units, depth)

    def partial_sums(first):
        return pl.pallas_call(
            lambda *refs: down_kernel(first, *refs),
            out_shape=jax.ShapeDtypeStruct((gy_count // 2, total_tokens, width), BF16),
            in_specs=[smem(), vmem(), vmem()],
            out_specs=vmem(),
            compiler_params=params(),
            name="down",
        )(ids, hidden, down)

    far_terms = partial_sums(1)
    near = swap(far_terms, "gy", 1)
    own_terms = partial_sums(0)
    summed = own_terms.astype(F32) + near.astype(F32)
    total = summed[0]
    for place in range(1, gy_count // 2):
        total = total + swap(summed[place].astype(BF16), "gy", 2 * place).astype(F32)
    total = total.reshape(gx_count, rows, width)
    result = stream.astype(F32) + total[0]
    for mask in range(1, gx_count):
        result = result + swap(total[mask].astype(BF16), "gx", mask).astype(F32)
    return (result.astype(BF16), compacted)


def gather_gy(value):
    count = lax.axis_size("gy")
    even = [value] + [swap(value, "gy", mask) for mask in range(2, count, 2)]
    pieces = []
    for one in even:
        pieces += [one, swap(one, "gy", 1)]
    return pieces


def solution(mesh):
    placed = (
        P("gx", "gy"),
        P(),
        P("gx", None, "gy"),
        P("gx", "gy"),
        P("gx", None, None, "gy"),
        P("gx"),
        P("gx"),
        P("gx", None),
        P("gx", None),
        P(),
        P("gy", None, None, "gx"),
        P("gy", "gx", None),
        P(),
        P(),
    )
    return jax.shard_map(
        per_device,
        mesh=mesh,
        in_specs=placed,
        out_specs=(P("gx", "gy"), P("gx", None, "gy")),
        check_vma=False,
    )
```

```python
import math

import jax
import jax.numpy as jnp
from jax import lax
from jax.experimental import pallas as pl
from jax.experimental.pallas import tpu as pltpu
from jax.sharding import PartitionSpec as P

HD = 128
CACHE_BLOCK = 2048
VMEM_LIMIT = 56 * 1024 * 1024
BF16 = jnp.bfloat16
F32 = jnp.float32


def vmem():
    return pl.BlockSpec(memory_space=pltpu.VMEM)


def smem():
    return pl.BlockSpec(memory_space=pltpu.SMEM)


def params():
    return pltpu.CompilerParams(vmem_limit_bytes=VMEM_LIMIT)


def swap(value, axis, mask):
    count = lax.axis_size(axis)
    return lax.ppermute(value, axis, [(one, one ^ mask) for one in range(count)])


def cost(flops, size):
    return pl.CostEstimate(flops=flops, bytes_accessed=size, transcendentals=0)


def ancestor_table(parents):
    nodes = parents.shape[-1]
    column = jnp.arange(nodes, dtype=jnp.int32)
    reach = (parents[:, :, None] == column[None, None, :]).astype(F32)
    reach = reach + jnp.eye(nodes, dtype=F32)[None]
    for _ in range((nodes - 1).bit_length()):
        reach = jnp.minimum(jnp.einsum("rij,rjk->rik", reach, reach), 1.0)
    return reach


def project_kernel(count, ids, gain, weight, *refs):
    pieces, outs, scaled = refs[:count], refs[count:-1], refs[-1]
    me_x, me_y = ids[0], ids[1]
    rows, width = pieces[0].shape
    share = scaled.shape[1] // width
    for mask, piece in enumerate(pieces):
        source = me_y ^ mask
        block, part = source // share, source % share
        columns = pl.ds(pl.multiple_of((me_x * share + part) * width, width), width)
        value = (piece[...].astype(F32) * gain[:, columns]).astype(BF16)
        scaled[
            pl.ds(pl.multiple_of(block * rows, rows), rows),
            pl.ds(pl.multiple_of(part * width, width), width),
        ] = value
    blocks = len(outs) // 2
    for mask in range(blocks):
        place = pl.ds(pl.multiple_of((me_x ^ mask) * rows, rows), rows)
        for which in range(3):
            value = jnp.dot(scaled[place, :], weight[which], preferred_element_type=F32)
            if which == 0:
                outs[mask][...] = value.astype(outs[mask].dtype)
            else:
                out = outs[blocks + mask]
                out[which - 1] = value.astype(out.dtype)


def blocked_query(query, request, draft, heads):
    rows = query[request * draft : (request + 1) * draft, :]
    if heads == 1:
        return rows
    column = lax.broadcasted_iota(jnp.int32, rows.shape, 1) // HD
    return jnp.concatenate(
        [jnp.where(column == head, rows, jnp.zeros_like(rows)) for head in range(heads)], axis=0
    )


def cache_kernel(
    requests, draft, heads, parts, lengths, owner, scale_of, *refs
):
    terms, (cache, top, mass, mixed, query, wide) = refs[:parts], refs[parts:]
    group, block = pl.program_id(0), pl.program_id(1)
    slots = cache.shape[2]

    @pl.when((group == 0) & (block == 0))
    def _():
        top[...] = jnp.full(top.shape, -jnp.inf, F32)
        mass[...] = jnp.zeros(mass.shape, F32)
        mixed[...] = jnp.zeros(mixed.shape, F32)
        total = terms[0][...]
        for term in terms[1:]:
            total = total + term[...].astype(F32)
        query[...] = (total * scale_of[...]).astype(BF16)
        for request in range(requests):
            wide[request] = blocked_query(query[...], request, draft, heads)

    left = lengths[group] - block * slots
    scale = 1.0 / math.sqrt(HD)
    for request in range(requests):

        @pl.when((owner[request] == group) & (left > 0))
        def _():
            scores = (
                lax.dot_general(
                    wide[request],
                    cache[0, 0],
                    (((1,), (1,)), ((), ())),
                    preferred_element_type=F32,
                )
                * scale
            )
            column = lax.broadcasted_iota(jnp.int32, scores.shape, 1)
            scores = jnp.where(column < left, scores, -jnp.inf)
            before = top[request]
            now = jnp.maximum(before, jnp.max(scores, axis=1, keepdims=True))
            powered = jnp.exp(scores - now[:, :1])
            fade = jnp.exp(before - now)
            top[request] = now
            mass[request] = mass[request] * fade + jnp.sum(powered, axis=1, keepdims=True)
            mixed[request] = mixed[request] * fade[:, :1] + jnp.dot(
                powered.astype(BF16), cache[0, 1], preferred_element_type=F32
            )


def draft_kernel(requests, draft, heads, parts, scale_of, *refs):
    pairs = refs[:parts]
    query, reach, rows, top, mass, mixed, attended, picked, key, value = refs[parts:]
    for which, kept in ((0, key), (1, value)):
        total = pairs[0][which]
        for pair in pairs[1:]:
            total = total + pair[which].astype(F32)
        kept[...] = (total * scale_of[...]).astype(BF16)
    tokens = key.shape[0]
    chosen = (
        lax.broadcasted_iota(jnp.int32, (rows.shape[0], tokens), 1) == rows[...]
    ).astype(BF16)
    picked[0] = jnp.dot(chosen, key[...], preferred_element_type=F32).astype(BF16)
    picked[1] = jnp.dot(chosen, value[...], preferred_element_type=F32).astype(BF16)
    scale = 1.0 / math.sqrt(HD)
    for request in range(requests):
        own = slice(request * draft, (request + 1) * draft)
        wide = blocked_query(query[...], request, draft, heads)
        scores = (
            lax.dot_general(
                wide, key[own, :], (((1,), (1,)), ((), ())), preferred_element_type=F32
            )
            * scale
        )
        seen = jnp.concatenate([reach[request]] * heads, axis=0)
        scores = jnp.where(seen > 0, scores, -jnp.inf)
        before = top[request][:, :1]
        now = jnp.maximum(before, jnp.max(scores, axis=1, keepdims=True))
        powered = jnp.exp(scores - now)
        fade = jnp.exp(before - now)
        sums = mass[request][:, :1] * fade + jnp.sum(powered, axis=1, keepdims=True)
        total = mixed[request] * fade + jnp.dot(
            powered.astype(BF16), value[own, :], preferred_element_type=F32
        )
        total = (total / sums).astype(BF16)
        for head in range(heads):
            attended[own, head * HD : (head + 1) * HD] = total[
                head * draft : (head + 1) * draft, head * HD : (head + 1) * HD
            ]


def output_kernel(count, ids, attended, output, *outs):
    me = ids[1]
    rows, width = outs[0].shape[-2:]
    for mask in range(count):
        place = pl.ds(pl.multiple_of((me ^ mask) * width, width), width)
        value = lax.dot_general(
            attended[...],
            output[place, :],
            (((1,), (1,)), ((), ())),
            preferred_element_type=F32,
        ).astype(BF16)
        outs[mask % 2][mask // 2] = value


def expert_kernel(count, unit, ids, gain, gates, weight, down, *refs):
    pieces, (odd, even, normed, total) = refs[:count], refs[count:]
    me_x, me_y = ids[0], ids[1]
    rows, width = pieces[0].shape
    step = pl.program_id(0)

    @pl.when(step == 0)
    def _():
        squares = jnp.zeros((rows, 1), F32)
        for piece in pieces:
            value = piece[...].astype(F32)
            squares = squares + jnp.sum(value * value, axis=1, keepdims=True)
        scale = lax.rsqrt(squares / (width * count) + 1e-05)
        for mask, piece in enumerate(pieces):
            columns = pl.ds(pl.multiple_of((me_y ^ mask) * width, width), width)
            value = piece[...].astype(F32) * scale * gain[:, columns]
            normed[:, columns] = value.astype(BF16)

    units = weight.shape[2] // 2
    both = jnp.dot(normed[...], weight[0], preferred_element_type=F32)
    gate, up = both[:, :units], both[:, units:]
    hidden = (gate / (1.0 + jnp.exp(-gate)) * up).astype(BF16)
    source = pl.ds(pl.multiple_of((me_x ^ unit) * rows, rows), rows)
    value = jnp.dot(hidden, down[0], preferred_element_type=F32) * gates[0, source, :]

    @pl.when(step == 0)
    def _():
        total[...] = value

    @pl.when(step > 0)
    def _():
        total[...] += value

    @pl.when(step == pl.num_programs(0) - 1)
    def _():
        for mask in range(count):
            columns = pl.ds(pl.multiple_of((me_y ^ mask) * width, width), width)
            (odd if mask % 2 else even)[mask // 2] = total[:, columns].astype(BF16)


def per_device(
    tokens,
    attention_gain,
    projection_weight,
    output_weight,
    prompt_cache,
    cache_length,
    prompt_group,
    parents,
    accepted_path,
    expert_gain,
    gate_up_weight,
    down_weight,
    route_experts,
    route_gates,
):
    gx_count, gy_count = lax.axis_size("gx"), lax.axis_size("gy")
    ids = jnp.stack([lax.axis_index("gx"), lax.axis_index("gy")]).astype(jnp.int32)
    rows, width = tokens.shape
    depth = attention_gain.shape[0]
    requests, draft = parents.shape
    groups = prompt_cache.shape[0]
    heads = width // HD

    output_full = lax.all_gather(output_weight, "gx", axis=0, tiled=True)

    wide_tokens = tokens.astype(F32)
    squares = jnp.sum(wide_tokens * wide_tokens, axis=1, keepdims=True)
    for bit in range(gy_count.bit_length() - 1):
        squares = squares + swap(squares, "gy", 1 << bit)
    row_scale = lax.rsqrt(squares / depth + 1e-05)

    share = gy_count // gx_count
    route = [
        (a * gy_count + b, (b // share) * gy_count + a * share + b % share)
        for a in range(gx_count)
        for b in range(gy_count)
    ]
    pieces = gather_gy(lax.ppermute(tokens, ("gx", "gy"), route))
    types = [F32] + [BF16] * (gx_count - 1)
    projected = pl.pallas_call(
        lambda *refs: project_kernel(gy_count, *refs),
        out_shape=[jax.ShapeDtypeStruct((rows, width), kind) for kind in types]
        + [jax.ShapeDtypeStruct((2, rows, width), kind) for kind in types],
        in_specs=[smem()] + [vmem()] * (2 + gy_count),
        out_specs=[vmem()] * (2 * gx_count),
        scratch_shapes=[pltpu.VMEM((gx_count * rows, share * width), BF16)],
        compiler_params=params(),
        name="project",
    )(
        ids, attention_gain.reshape(1, depth), jnp.transpose(projection_weight, (1, 0, 2)), *pieces
    )
    query_terms, pair_terms = projected[:gx_count], projected[gx_count:]
    query_terms = [query_terms[0]] + [
        swap(query_terms[mask], "gx", mask) for mask in range(1, gx_count)
    ]
    pair_terms = [pair_terms[0]] + [
        swap(pair_terms[mask], "gx", mask) for mask in range(1, gx_count)
    ]

    experts = gate_up_weight.shape[0]
    units = gate_up_weight.shape[3]
    gate_up = gate_up_weight.reshape(experts, depth, 2 * units)
    gate_up, query_terms[0] = lax.optimization_barrier((gate_up, query_terms[0]))

    slots = prompt_cache.shape[2]
    step = min(CACHE_BLOCK, slots)
    wide_rows = heads * draft
    constant = lambda *_: (0, 0, 0)
    flat = lambda *_: (0, 0)
    top, mass, mixed, query = pl.pallas_call(
        lambda *refs: cache_kernel(requests, draft, heads, gx_count, *refs),
        grid_spec=pltpu.PrefetchScalarGridSpec(
            num_scalar_prefetch=2,
            grid=(groups, slots // step),
            in_specs=[pl.BlockSpec((rows, 1), flat)]
            + [pl.BlockSpec((rows, width), flat)] * gx_count
            + [
                pl.BlockSpec(
                    (1, 2, step, width),
                    lambda group, block, lengths, owner: (
                        group,
                        0,
                        jnp.minimum(block, (lengths[group] - 1) // step),
                        0,
                    ),
                ),
            ],
            out_specs=[
                pl.BlockSpec((requests, wide_rows, HD), constant),
                pl.BlockSpec((requests, wide_rows, HD), constant),
                pl.BlockSpec((requests, wide_rows, width), constant),
                pl.BlockSpec((rows, width), flat),
            ],
            scratch_shapes=[pltpu.VMEM((requests, wide_rows, width), BF16)],
        ),
        out_shape=(
            jax.ShapeDtypeStruct((requests, wide_rows, HD), F32),
            jax.ShapeDtypeStruct((requests, wide_rows, HD), F32),
            jax.ShapeDtypeStruct((requests, wide_rows, width), F32),
            jax.ShapeDtypeStruct((rows, width), BF16),
        ),
        compiler_params=params(),
        cost_estimate=cost(20 * rows * slots * width, 4 * groups * slots * width),
        name="cache",
    )(cache_length, prompt_group % groups, row_scale, *query_terms, prompt_cache)

    accepted = accepted_path.shape[1]
    chosen = (jnp.arange(requests, dtype=jnp.int32)[:, None] * draft + accepted_path).reshape(-1, 1)
    attended, picked = pl.pallas_call(
        lambda *refs: draft_kernel(requests, draft, heads, gx_count, *refs),
        out_shape=(
            jax.ShapeDtypeStruct((rows, width), BF16),
            jax.ShapeDtypeStruct((2, requests * accepted, width), BF16),
        ),
        in_specs=[vmem()] * (gx_count + 7),
        out_specs=(vmem(), vmem()),
        scratch_shapes=[
            pltpu.VMEM((rows, width), BF16),
            pltpu.VMEM((rows, width), BF16),
        ],
        compiler_params=params(),
        name="draft",
    )(row_scale, *pair_terms, query, ancestor_table(parents), chosen, top, mass, mixed)
    compacted = jnp.transpose(picked, (1, 0, 2))

    half = jax.ShapeDtypeStruct((gy_count // 2, rows, width), BF16)
    even, odd = pl.pallas_call(
        lambda *refs: output_kernel(gy_count, *refs),
        out_shape=(half, half),
        in_specs=[smem(), vmem(), vmem()],
        out_specs=(vmem(), vmem()),
        compiler_params=params(),
        name="output",
    )(ids, attended, output_full)

    summed = even.astype(F32) + swap(odd, "gy", 1).astype(F32)
    stream = tokens.astype(F32) + summed[0]
    for place in range(1, gy_count // 2):
        stream = stream + swap(summed[place].astype(BF16), "gy", 2 * place).astype(F32)
    stream = stream.astype(BF16)

    expert_ids = lax.axis_index("gy") * experts + jnp.arange(experts, dtype=jnp.int32)
    hit = route_experts[None] == expert_ids[:, None, None]
    gates = jnp.sum(jnp.where(hit, route_gates.astype(F32)[None], 0.0), axis=2)[:, :, None]
    result = stream.astype(F32)
    for unit in range(gx_count):
        one = stream if unit == 0 else swap(stream, "gx", unit)
        everything = double_gy(one, unit % 2)
        odd, even = pl.pallas_call(
            lambda *refs: expert_kernel(gy_count, unit, *refs),
            grid=(experts,),
            in_specs=[
                smem(),
                pl.BlockSpec((1, depth), lambda expert: (0, 0)),
                pl.BlockSpec((1, gx_count * rows, 1), lambda expert: (expert, 0, 0)),
                pl.BlockSpec((1, depth, 2 * units), lambda expert: (expert, 0, 0)),
                pl.BlockSpec((1, units, depth), lambda expert: (expert, 0, 0)),
            ]
            + [vmem()] * gy_count,
            out_specs=[vmem(), vmem()],
            out_shape=(half, half),
            scratch_shapes=[pltpu.VMEM((rows, depth), BF16), pltpu.VMEM((rows, depth), F32)],
            compiler_params=params(),
            cost_estimate=cost(
                6 * rows * depth * experts * units, 6 * depth * experts * units
            ),
            name="experts",
        )(ids, expert_gain.reshape(1, depth), gates, gate_up, down_weight, *everything)
        summed = even.astype(F32) + swap(odd, "gy", 1).astype(F32)
        total = halve_gy(summed, unit % 2)
        if unit:
            total = swap(total.astype(BF16), "gx", unit).astype(F32)
        result = result + total
    return (result.astype(BF16), compacted)


def gather_gy(value):
    count = lax.axis_size("gy")
    even = [value] + [swap(value, "gy", mask) for mask in range(2, count, 2)]
    pieces = []
    for one in even:
        pieces += [one, swap(one, "gy", 1)]
    return pieces


def far_bits(turn):
    bits = list(range(1, lax.axis_size("gy").bit_length() - 1))
    return bits[::-1] if turn else bits


def double_gy(value, turn):
    held = {0: value}
    for bit in far_bits(turn):
        held.update({mask | 1 << bit: swap(one, "gy", 1 << bit) for mask, one in held.items()})
    held.update({mask | 1: swap(one, "gy", 1) for mask, one in held.items()})
    return [held[mask] for mask in range(len(held))]


def halve_gy(value, turn):
    held = [(2 * place, value[place]) for place in range(value.shape[0])]
    for bit in far_bits(turn):
        mine = [(mask, one) for mask, one in held if not mask >> bit & 1]
        sent = jnp.stack([one for mask, one in held if mask >> bit & 1]).astype(BF16)
        got = swap(sent, "gy", 1 << bit).astype(F32)
        held = [(mask, one + got[place]) for place, (mask, one) in enumerate(mine)]
    return held[0][1]


def solution(mesh):
    placed = (
        P("gx", "gy"),
        P(),
        P("gx", None, "gy"),
        P("gx", "gy"),
        P("gx", None, None, "gy"),
        P("gx"),
        P("gx"),
        P("gx", None),
        P("gx", None),
        P(),
        P("gy", None, None, "gx"),
        P("gy", "gx", None),
        P(),
        P(),
    )
    return jax.shard_map(
        per_device,
        mesh=mesh,
        in_specs=placed,
        out_specs=(P("gx", "gy"), P("gx", None, "gy")),
        check_vma=False,
    )
```

```python
import math

import jax
import jax.numpy as jnp
from jax import lax
from jax.experimental import pallas as pl
from jax.experimental.pallas import tpu as pltpu
from jax.sharding import PartitionSpec as P

HD = 128
CACHE_BLOCK = 1024
VMEM_LIMIT = 56 * 1024 * 1024
BF16 = jnp.bfloat16
F32 = jnp.float32
EXPONENT = math.log2(math.e) / math.sqrt(HD)


def vmem():
    return pl.BlockSpec(memory_space=pltpu.VMEM)


def smem():
    return pl.BlockSpec(memory_space=pltpu.SMEM)


def params():
    return pltpu.CompilerParams(vmem_limit_bytes=VMEM_LIMIT)


def swap(value, axis, mask):
    count = lax.axis_size(axis)
    return lax.ppermute(value, axis, [(one, one ^ mask) for one in range(count)])


def cost(flops, size):
    return pl.CostEstimate(flops=flops, bytes_accessed=size, transcendentals=0)


def ancestor_table(parents):
    nodes = parents.shape[-1]
    column = jnp.arange(nodes, dtype=jnp.int32)
    reach = (parents[:, :, None] == column[None, None, :]).astype(F32)
    reach = reach + jnp.eye(nodes, dtype=F32)[None]
    for _ in range((nodes - 1).bit_length()):
        reach = jnp.minimum(jnp.einsum("rij,rjk->rik", reach, reach), 1.0)
    return reach


def project_kernel(count, ids, gain, weight, *refs):
    pieces, outs, scaled = refs[:count], refs[count:-1], refs[-1]
    me_x, me_y = ids[0], ids[1]
    rows, width = pieces[0].shape
    share = scaled.shape[1] // width
    for mask, piece in enumerate(pieces):
        source = me_y ^ mask
        block, part = source // share, source % share
        columns = pl.ds(pl.multiple_of((me_x * share + part) * width, width), width)
        value = (piece[...].astype(F32) * gain[:, columns]).astype(BF16)
        scaled[
            pl.ds(pl.multiple_of(block * rows, rows), rows),
            pl.ds(pl.multiple_of(part * width, width), width),
        ] = value
    blocks = len(outs) // 2
    for mask in range(blocks):
        place = pl.ds(pl.multiple_of((me_x ^ mask) * rows, rows), rows)
        for which in range(3):
            value = jnp.dot(scaled[place, :], weight[which], preferred_element_type=F32)
            if which == 0:
                outs[mask][...] = value.astype(outs[mask].dtype)
            else:
                out = outs[blocks + mask]
                out[which - 1] = value.astype(out.dtype)


def blocked_query(query, request, draft, heads):
    rows = query[request * draft : (request + 1) * draft, :]
    if heads == 1:
        return rows
    column = lax.broadcasted_iota(jnp.int32, rows.shape, 1) // HD
    return jnp.concatenate(
        [jnp.where(column == head, rows, jnp.zeros_like(rows)) for head in range(heads)], axis=0
    )


def cache_kernel(
    requests, draft, heads, parts, lengths, first, held, place, scale_of, *refs
):
    terms, (cache, top, mass, mixed, query, wide) = refs[:parts], refs[parts:]
    group, block = pl.program_id(0), pl.program_id(1)
    slots = cache.shape[2]
    size = heads * draft

    @pl.when((group == 0) & (block == 0))
    def _():
        top[...] = jnp.full(top.shape, -jnp.inf, F32)
        mass[...] = jnp.zeros(mass.shape, F32)
        mixed[...] = jnp.zeros(mixed.shape, F32)
        total = terms[0][...]
        for term in terms[1:]:
            total = total + term[...].astype(F32)
        query[...] = (total * scale_of[...]).astype(BF16)
        for request in range(requests):
            rows = pl.ds(pl.multiple_of(place[request] * size, size), size)
            wide[rows, :] = blocked_query(query[...], request, draft, heads)

    left = lengths[group] - block * slots
    for count in range(1, requests + 1):

        @pl.when((held[group] == count) & (left > 0))
        def _():
            rows = pl.ds(pl.multiple_of(first[group] * size, size), count * size)
            scores = lax.dot_general(
                wide[rows, :],
                cache[0, 0],
                (((1,), (1,)), ((), ())),
                preferred_element_type=F32,
            )
            column = lax.broadcasted_iota(jnp.int32, (1, slots), 1)
            scores = scores + jnp.where(column < left, 0.0, -jnp.inf)
            before = top[rows, :]
            now = jnp.maximum(before, jnp.max(scores, axis=1, keepdims=True))
            powered = jnp.exp2((scores - now[:, :1]) * EXPONENT)
            fade = jnp.exp2((before - now) * EXPONENT)
            top[rows, :] = now
            mass[rows, :] = mass[rows, :] * fade + jnp.sum(powered, axis=1, keepdims=True)
            mixed[rows, :] = mixed[rows, :] * fade[:, :1] + jnp.dot(
                powered.astype(BF16), cache[0, 1], preferred_element_type=F32
            )


def draft_kernel(requests, draft, heads, parts, place, scale_of, *refs):
    pairs = refs[:parts]
    query, reach, rows, top, mass, mixed, attended, picked, key, value = refs[parts:]
    for which, kept in ((0, key), (1, value)):
        total = pairs[0][which]
        for pair in pairs[1:]:
            total = total + pair[which].astype(F32)
        kept[...] = (total * scale_of[...]).astype(BF16)
    tokens = key.shape[0]
    chosen = (
        lax.broadcasted_iota(jnp.int32, (rows.shape[0], tokens), 1) == rows[...]
    ).astype(BF16)
    picked[0] = jnp.dot(chosen, key[...], preferred_element_type=F32).astype(BF16)
    picked[1] = jnp.dot(chosen, value[...], preferred_element_type=F32).astype(BF16)
    size = heads * draft
    for request in range(requests):
        own = slice(request * draft, (request + 1) * draft)
        kept = pl.ds(pl.multiple_of(place[request] * size, size), size)
        wide = blocked_query(query[...], request, draft, heads)
        scores = lax.dot_general(
            wide, key[own, :], (((1,), (1,)), ((), ())), preferred_element_type=F32
        )
        seen = jnp.concatenate([reach[request]] * heads, axis=0)
        scores = jnp.where(seen > 0, scores, -jnp.inf)
        before = top[kept, :][:, :1]
        now = jnp.maximum(before, jnp.max(scores, axis=1, keepdims=True))
        powered = jnp.exp2((scores - now) * EXPONENT)
        fade = jnp.exp2((before - now) * EXPONENT)
        sums = mass[kept, :][:, :1] * fade + jnp.sum(powered, axis=1, keepdims=True)
        total = mixed[kept, :] * fade + jnp.dot(
            powered.astype(BF16), value[own, :], preferred_element_type=F32
        )
        total = (total / sums).astype(BF16)
        for head in range(heads):
            attended[own, head * HD : (head + 1) * HD] = total[
                head * draft : (head + 1) * draft, head * HD : (head + 1) * HD
            ]


def output_kernel(count, ids, attended, output, *outs):
    me = ids[1]
    rows, width = outs[0].shape[-2:]
    for mask in range(count):
        place = pl.ds(pl.multiple_of((me ^ mask) * width, width), width)
        value = lax.dot_general(
            attended[...],
            output[place, :],
            (((1,), (1,)), ((), ())),
            preferred_element_type=F32,
        ).astype(BF16)
        outs[mask % 2][mask // 2] = value


def expert_kernel(count, masks, ids, gain, gates, weight, down, *refs):
    blocks = len(masks)
    pieces, outs, (normed, total) = refs[: blocks * count], refs[blocks * count : -2], refs[-2:]
    me_x, me_y = ids[0], ids[1]
    rows, width = pieces[0].shape
    step = pl.program_id(0)

    @pl.when(step == 0)
    def _():
        for block in range(blocks):
            own = pieces[block * count : (block + 1) * count]
            place = slice(block * rows, (block + 1) * rows)
            squares = jnp.zeros((rows, 1), F32)
            for piece in own:
                value = piece[...].astype(F32)
                squares = squares + jnp.sum(value * value, axis=1, keepdims=True)
            scale = lax.rsqrt(squares / (width * count) + 1e-05)
            for mask, piece in enumerate(own):
                columns = pl.ds(pl.multiple_of((me_y ^ mask) * width, width), width)
                value = piece[...].astype(F32) * scale * gain[:, columns]
                normed[place, columns] = value.astype(BF16)

    units = weight.shape[2] // 2
    both = jnp.dot(normed[...], weight[0], preferred_element_type=F32)
    gate, up = both[:, :units], both[:, units:]
    hidden = (gate / (1.0 + jnp.exp(-gate)) * up).astype(BF16)
    value = jnp.dot(hidden, down[0], preferred_element_type=F32)
    for block, mask in enumerate(masks):
        place = slice(block * rows, (block + 1) * rows)
        source = pl.ds(pl.multiple_of((me_x ^ mask) * rows, rows), rows)
        part = value[place, :] * gates[0, source, :]

        @pl.when(step == 0)
        def _():
            total[place, :] = part

        @pl.when(step > 0)
        def _():
            total[place, :] += part

    @pl.when(step == pl.num_programs(0) - 1)
    def _():
        for block in range(blocks):
            place = slice(block * rows, (block + 1) * rows)
            for mask in range(count):
                columns = pl.ds(pl.multiple_of((me_y ^ mask) * width, width), width)
                outs[2 * block + mask % 2][mask // 2] = total[place, columns].astype(BF16)


def per_device(
    tokens,
    attention_gain,
    projection_weight,
    output_weight,
    prompt_cache,
    cache_length,
    prompt_group,
    parents,
    accepted_path,
    expert_gain,
    gate_up_weight,
    down_weight,
    route_experts,
    route_gates,
):
    gx_count, gy_count = lax.axis_size("gx"), lax.axis_size("gy")
    ids = jnp.stack([lax.axis_index("gx"), lax.axis_index("gy")]).astype(jnp.int32)
    rows, width = tokens.shape
    depth = attention_gain.shape[0]
    requests, draft = parents.shape
    groups = prompt_cache.shape[0]
    heads = width // HD

    output_full = lax.all_gather(output_weight, "gx", axis=0, tiled=True)

    wide_tokens = tokens.astype(F32)
    squares = jnp.sum(wide_tokens * wide_tokens, axis=1, keepdims=True)
    for bit in range(gy_count.bit_length() - 1):
        squares = squares + swap(squares, "gy", 1 << bit)
    row_scale = lax.rsqrt(squares / depth + 1e-05)

    share = gy_count // gx_count
    route = [
        (a * gy_count + b, (b // share) * gy_count + a * share + b % share)
        for a in range(gx_count)
        for b in range(gy_count)
    ]
    moved = lax.ppermute(tokens, ("gx", "gy"), route)
    experts = gate_up_weight.shape[0]
    units = gate_up_weight.shape[3]
    gate_up = gate_up_weight.reshape(experts, depth, 2 * units)
    gate_up, moved = lax.optimization_barrier((gate_up, moved))
    pieces = gather_gy(moved)
    types = [F32] + [BF16] * (gx_count - 1)
    projected = pl.pallas_call(
        lambda *refs: project_kernel(gy_count, *refs),
        out_shape=[jax.ShapeDtypeStruct((rows, width), kind) for kind in types]
        + [jax.ShapeDtypeStruct((2, rows, width), kind) for kind in types],
        in_specs=[smem()] + [vmem()] * (2 + gy_count),
        out_specs=[vmem()] * (2 * gx_count),
        scratch_shapes=[pltpu.VMEM((gx_count * rows, share * width), BF16)],
        compiler_params=params(),
        name="project",
    )(
        ids, attention_gain.reshape(1, depth), jnp.transpose(projection_weight, (1, 0, 2)), *pieces
    )
    query_terms, pair_terms = projected[:gx_count], projected[gx_count:]
    query_terms = [query_terms[0]] + [
        swap(query_terms[mask], "gx", mask) for mask in range(1, gx_count)
    ]
    pair_terms = [pair_terms[0]] + [
        swap(pair_terms[mask], "gx", mask) for mask in range(1, gx_count)
    ]

    owner = prompt_group % groups
    order = jnp.arange(requests, dtype=jnp.int32)
    ahead = (owner[None, :] < owner[:, None]) | (
        (owner[None, :] == owner[:, None]) & (order[None, :] < order[:, None])
    )
    place = jnp.sum(ahead.astype(jnp.int32), axis=1)
    group_ids = jnp.arange(groups, dtype=jnp.int32)
    held = jnp.sum((owner[None, :] == group_ids[:, None]).astype(jnp.int32), axis=1)
    first = jnp.sum((owner[None, :] < group_ids[:, None]).astype(jnp.int32), axis=1)

    slots = prompt_cache.shape[2]
    step = min(CACHE_BLOCK, slots)
    wide_rows = heads * draft
    flat = lambda *_: (0, 0)
    top, mass, mixed, query = pl.pallas_call(
        lambda *refs: cache_kernel(requests, draft, heads, gx_count, *refs),
        grid_spec=pltpu.PrefetchScalarGridSpec(
            num_scalar_prefetch=4,
            grid=(groups, slots // step),
            in_specs=[pl.BlockSpec((rows, 1), flat)]
            + [pl.BlockSpec((rows, width), flat)] * gx_count
            + [
                pl.BlockSpec(
                    (1, 2, step, width),
                    lambda group, block, lengths, first, held, place: (
                        group,
                        0,
                        jnp.where(
                            held[group] > 0, jnp.minimum(block, (lengths[group] - 1) // step), 0
                        ),
                        0,
                    ),
                ),
            ],
            out_specs=[
                pl.BlockSpec((requests * wide_rows, HD), flat),
                pl.BlockSpec((requests * wide_rows, HD), flat),
                pl.BlockSpec((requests * wide_rows, width), flat),
                pl.BlockSpec((rows, width), flat),
            ],
            scratch_shapes=[pltpu.VMEM((requests * wide_rows, width), BF16)],
        ),
        out_shape=(
            jax.ShapeDtypeStruct((requests * wide_rows, HD), F32),
            jax.ShapeDtypeStruct((requests * wide_rows, HD), F32),
            jax.ShapeDtypeStruct((requests * wide_rows, width), F32),
            jax.ShapeDtypeStruct((rows, width), BF16),
        ),
        compiler_params=params(),
        cost_estimate=cost(20 * rows * slots * width, 4 * groups * slots * width),
        name="cache",
    )(cache_length, first, held, place, row_scale, *query_terms, prompt_cache)

    accepted = accepted_path.shape[1]
    chosen = (jnp.arange(requests, dtype=jnp.int32)[:, None] * draft + accepted_path).reshape(-1, 1)
    attended, picked = pl.pallas_call(
        lambda *refs: draft_kernel(requests, draft, heads, gx_count, *refs),
        out_shape=(
            jax.ShapeDtypeStruct((rows, width), BF16),
            jax.ShapeDtypeStruct((2, requests * accepted, width), BF16),
        ),
        in_specs=[smem()] + [vmem()] * (gx_count + 7),
        out_specs=(vmem(), vmem()),
        scratch_shapes=[
            pltpu.VMEM((rows, width), BF16),
            pltpu.VMEM((rows, width), BF16),
        ],
        compiler_params=params(),
        name="draft",
    )(place, row_scale, *pair_terms, query, ancestor_table(parents), chosen, top, mass, mixed)
    compacted = jnp.transpose(picked, (1, 0, 2))

    half = jax.ShapeDtypeStruct((gy_count // 2, rows, width), BF16)
    even, odd = pl.pallas_call(
        lambda *refs: output_kernel(gy_count, *refs),
        out_shape=(half, half),
        in_specs=[smem(), vmem(), vmem()],
        out_specs=(vmem(), vmem()),
        compiler_params=params(),
        name="output",
    )(ids, attended, output_full)

    summed = even.astype(F32) + swap(odd, "gy", 1).astype(F32)
    stream = tokens.astype(F32) + summed[0]
    for place in range(1, gy_count // 2):
        stream = stream + swap(summed[place].astype(BF16), "gy", 2 * place).astype(F32)
    stream = stream.astype(BF16)

    expert_ids = lax.axis_index("gy") * experts + jnp.arange(experts, dtype=jnp.int32)
    hit = route_experts[None] == expert_ids[:, None, None]
    gates = jnp.sum(jnp.where(hit, route_gates.astype(F32)[None], 0.0), axis=2)[:, :, None]
    blocks = [stream] + [swap(stream, "gx", mask) for mask in range(1, gx_count)]
    together = 2
    everything = [double_gy(one, mask % 2) for mask, one in enumerate(blocks[:together])]
    result = stream.astype(F32)
    pending, waiting = [], []
    for start in range(0, gx_count, together):
        masks = range(start, start + together)
        inputs = [one for pieces in everything for one in pieces]
        after = blocks[start + together : start + 2 * together]
        inputs, waiting, after = lax.optimization_barrier((inputs, waiting, after))
        far = [gather_far(one) for one in after]
        arrived = [send_far(one) for one in waiting]
        terms = pl.pallas_call(
            lambda *refs: expert_kernel(gy_count, masks, *refs),
            grid=(experts,),
            in_specs=[
                smem(),
                pl.BlockSpec((1, depth), lambda expert: (0, 0)),
                pl.BlockSpec((1, gx_count * rows, 1), lambda expert: (expert, 0, 0)),
                pl.BlockSpec((1, depth, 2 * units), lambda expert: (expert, 0, 0)),
                pl.BlockSpec((1, units, depth), lambda expert: (expert, 0, 0)),
            ]
            + [vmem()] * (together * gy_count),
            out_specs=[vmem()] * (2 * together),
            out_shape=[half] * (2 * together),
            scratch_shapes=[
                pltpu.VMEM((together * rows, depth), BF16),
                pltpu.VMEM((together * rows, depth), F32),
            ],
            compiler_params=params(),
            cost_estimate=cost(
                6 * together * rows * depth * experts * units, 6 * depth * experts * units
            ),
            name="experts",
        )(ids, expert_gain.reshape(1, depth), gates, gate_up, down_weight, *inputs)
        terms, far, arrived = lax.optimization_barrier((terms, far, arrived))
        pending += [
            (start - together + place, sum([one.astype(F32) for one in got], held[0]))
            for place, (held, got) in enumerate(zip(waiting, arrived))
        ]
        near = [swap(odd, "gy", 1) for odd in terms[1::2]]
        everything = [gather_near(one) for one in far]
        waiting = []
        for mask, even, odd in zip(masks, terms[0::2], near):
            summed = even.astype(F32) + odd.astype(F32)
            if start + together < gx_count:
                waiting.append([summed[0]] + [one.astype(BF16) for one in summed[1:]])
            else:
                pending.append((mask, halve_gy(summed, mask % 2)))
    for mask, total in pending:
        if mask:
            total = swap(total.astype(BF16), "gx", mask).astype(F32)
        result = result + total
    return (result.astype(BF16), compacted)


def send_far(held):
    return [swap(one, "gy", 2 * place) for place, one in enumerate(held) if place]


def gather_far(value):
    return [value] + [swap(value, "gy", mask) for mask in range(2, lax.axis_size("gy"), 2)]


def gather_near(even):
    return [one for held in even for one in (held, swap(held, "gy", 1))]


def gather_gy(value):
    return gather_near(gather_far(value))


def far_bits(turn):
    bits = list(range(1, lax.axis_size("gy").bit_length() - 1))
    return bits[::-1] if turn else bits


def double_gy(value, turn):
    held = {0: value}
    for bit in far_bits(turn):
        held.update({mask | 1 << bit: swap(one, "gy", 1 << bit) for mask, one in held.items()})
    held.update({mask | 1: swap(one, "gy", 1) for mask, one in held.items()})
    return [held[mask] for mask in range(len(held))]


def halve_gy(value, turn):
    held = [(2 * place, value[place]) for place in range(value.shape[0])]
    for bit in far_bits(turn):
        mine = [(mask, one) for mask, one in held if not mask >> bit & 1]
        sent = jnp.stack([one for mask, one in held if mask >> bit & 1]).astype(BF16)
        got = swap(sent, "gy", 1 << bit).astype(F32)
        held = [(mask, one + got[place]) for place, (mask, one) in enumerate(mine)]
    return held[0][1]


def solution(mesh):
    placed = (
        P("gx", "gy"),
        P(),
        P("gx", None, "gy"),
        P("gx", "gy"),
        P("gx", None, None, "gy"),
        P("gx"),
        P("gx"),
        P("gx", None),
        P("gx", None),
        P(),
        P("gy", None, None, "gx"),
        P("gy", "gx", None),
        P(),
        P(),
    )
    return jax.shard_map(
        per_device,
        mesh=mesh,
        in_specs=placed,
        out_specs=(P("gx", "gy"), P("gx", None, "gy")),
        check_vma=False,
    )
```

```python
import math

import jax
import jax.numpy as jnp
from jax import lax
from jax.experimental import pallas as pl
from jax.experimental.pallas import tpu as pltpu
from jax.sharding import PartitionSpec as P

HD = 128
CACHE_BLOCK = 1024
VMEM_LIMIT = 56 * 1024 * 1024
BF16 = jnp.bfloat16
F32 = jnp.float32
EXPONENT = math.log2(math.e) / math.sqrt(HD)


def vmem():
    return pl.BlockSpec(memory_space=pltpu.VMEM)


def smem():
    return pl.BlockSpec(memory_space=pltpu.SMEM)


def params():
    return pltpu.CompilerParams(vmem_limit_bytes=VMEM_LIMIT)


def swap(value, axis, mask):
    count = lax.axis_size(axis)
    return lax.ppermute(value, axis, [(one, one ^ mask) for one in range(count)])


def cost(flops, size):
    return pl.CostEstimate(flops=flops, bytes_accessed=size, transcendentals=0)


def ancestor_table(parents):
    nodes = parents.shape[-1]
    column = jnp.arange(nodes, dtype=jnp.int32)
    reach = (parents[:, :, None] == column[None, None, :]).astype(F32)
    reach = reach + jnp.eye(nodes, dtype=F32)[None]
    for _ in range((nodes - 1).bit_length()):
        reach = jnp.minimum(jnp.einsum("rij,rjk->rik", reach, reach), 1.0)
    return reach


def project_kernel(count, ids, gain, weight, *refs):
    pieces, outs, scaled = refs[:count], refs[count:-1], refs[-1]
    me_x, me_y = ids[0], ids[1]
    rows, width = pieces[0].shape
    share = scaled.shape[1] // width
    for mask, piece in enumerate(pieces):
        source = me_y ^ mask
        block, part = source // share, source % share
        columns = pl.ds(pl.multiple_of((me_x * share + part) * width, width), width)
        value = (piece[...].astype(F32) * gain[:, columns]).astype(BF16)
        scaled[
            pl.ds(pl.multiple_of(block * rows, rows), rows),
            pl.ds(pl.multiple_of(part * width, width), width),
        ] = value
    blocks = len(outs) // 2
    for mask in range(blocks):
        place = pl.ds(pl.multiple_of((me_x ^ mask) * rows, rows), rows)
        for which in range(3):
            value = jnp.dot(scaled[place, :], weight[which], preferred_element_type=F32)
            if which == 0:
                outs[mask][...] = value.astype(outs[mask].dtype)
            else:
                out = outs[blocks + mask]
                out[which - 1] = value.astype(out.dtype)


def blocked_query(query, request, draft, heads):
    rows = query[request * draft : (request + 1) * draft, :]
    if heads == 1:
        return rows
    column = lax.broadcasted_iota(jnp.int32, rows.shape, 1) // HD
    return jnp.concatenate(
        [jnp.where(column == head, rows, jnp.zeros_like(rows)) for head in range(heads)], axis=0
    )


def cache_kernel(
    requests, draft, heads, parts, lengths, first, held, place, scale_of, *refs
):
    terms, (cache, top, mass, mixed, query, wide) = refs[:parts], refs[parts:]
    group, block = pl.program_id(0), pl.program_id(1)
    slots = cache.shape[2]
    size = heads * draft

    @pl.when((group == 0) & (block == 0))
    def _():
        top[...] = jnp.full(top.shape, -jnp.inf, F32)
        mass[...] = jnp.zeros(mass.shape, F32)
        mixed[...] = jnp.zeros(mixed.shape, F32)
        total = terms[0][...]
        for term in terms[1:]:
            total = total + term[...].astype(F32)
        query[...] = (total * scale_of[...]).astype(BF16)
        for request in range(requests):
            rows = pl.ds(pl.multiple_of(place[request] * size, size), size)
            wide[rows, :] = blocked_query(query[...], request, draft, heads)

    left = lengths[group] - block * slots
    for count in range(1, requests + 1):

        @pl.when((held[group] == count) & (left > 0))
        def _():
            rows = pl.ds(pl.multiple_of(first[group] * size, size), count * size)
            scores = lax.dot_general(
                wide[rows, :],
                cache[0, 0],
                (((1,), (1,)), ((), ())),
                preferred_element_type=F32,
            )
            column = lax.broadcasted_iota(jnp.int32, (1, slots), 1)
            scores = scores + jnp.where(column < left, 0.0, -jnp.inf)
            before = top[rows, :]
            now = jnp.maximum(before, jnp.max(scores, axis=1, keepdims=True))
            powered = jnp.exp2((scores - now[:, :1]) * EXPONENT)
            fade = jnp.exp2((before - now) * EXPONENT)
            top[rows, :] = now
            mass[rows, :] = mass[rows, :] * fade + jnp.sum(powered, axis=1, keepdims=True)
            mixed[rows, :] = mixed[rows, :] * fade[:, :1] + jnp.dot(
                powered.astype(BF16), cache[0, 1], preferred_element_type=F32
            )


def draft_kernel(requests, draft, heads, parts, place, scale_of, *refs):
    pairs = refs[:parts]
    query, reach, rows, top, mass, mixed, attended, picked, key, value = refs[parts:]
    for which, kept in ((0, key), (1, value)):
        total = pairs[0][which]
        for pair in pairs[1:]:
            total = total + pair[which].astype(F32)
        kept[...] = (total * scale_of[...]).astype(BF16)
    tokens = key.shape[0]
    chosen = (
        lax.broadcasted_iota(jnp.int32, (rows.shape[0], tokens), 1) == rows[...]
    ).astype(BF16)
    picked[0] = jnp.dot(chosen, key[...], preferred_element_type=F32).astype(BF16)
    picked[1] = jnp.dot(chosen, value[...], preferred_element_type=F32).astype(BF16)
    size = heads * draft
    for request in range(requests):
        own = slice(request * draft, (request + 1) * draft)
        kept = pl.ds(pl.multiple_of(place[request] * size, size), size)
        wide = blocked_query(query[...], request, draft, heads)
        scores = lax.dot_general(
            wide, key[own, :], (((1,), (1,)), ((), ())), preferred_element_type=F32
        )
        seen = jnp.concatenate([reach[request]] * heads, axis=0)
        scores = jnp.where(seen > 0, scores, -jnp.inf)
        before = top[kept, :][:, :1]
        now = jnp.maximum(before, jnp.max(scores, axis=1, keepdims=True))
        powered = jnp.exp2((scores - now) * EXPONENT)
        fade = jnp.exp2((before - now) * EXPONENT)
        sums = mass[kept, :][:, :1] * fade + jnp.sum(powered, axis=1, keepdims=True)
        total = mixed[kept, :] * fade + jnp.dot(
            powered.astype(BF16), value[own, :], preferred_element_type=F32
        )
        total = (total / sums).astype(BF16)
        for head in range(heads):
            attended[own, head * HD : (head + 1) * HD] = total[
                head * draft : (head + 1) * draft, head * HD : (head + 1) * HD
            ]


def output_kernel(count, ids, attended, output, *outs):
    me = ids[1]
    rows, width = outs[0].shape[-2:]
    for mask in range(count):
        place = pl.ds(pl.multiple_of((me ^ mask) * width, width), width)
        value = lax.dot_general(
            attended[...],
            output[place, :],
            (((1,), (1,)), ((), ())),
            preferred_element_type=F32,
        ).astype(BF16)
        outs[mask % 2][mask // 2] = value


def expert_kernel(count, masks, stacked, ids, gain, gates, gate_weight, up_weight, down, *refs):
    blocks = len(masks)
    pieces, (odd, even, normed, hidden, held, arrival) = refs[:-6], refs[-6:]
    me_x, me_y = ids[0], ids[1]
    rows, width = pieces[0].shape[-2:]
    step = pl.program_id(0)
    fetch = pltpu.make_async_copy(down, held, arrival)

    @pl.when(step == 0)
    def _():
        fetch.start()
        for block in range(blocks):
            if stacked:
                own = [piece.at[block] for piece in pieces]
            else:
                own = pieces[block * count : (block + 1) * count]
            place = slice(block * rows, (block + 1) * rows)
            squares = jnp.zeros((rows, 1), F32)
            for piece in own:
                value = piece[...].astype(F32)
                squares = squares + jnp.sum(value * value, axis=1, keepdims=True)
            scale = lax.rsqrt(squares / (width * count) + 1e-05)
            for mask, piece in enumerate(own):
                columns = pl.ds(pl.multiple_of((me_y ^ mask) * width, width), width)
                value = piece[...].astype(F32) * scale * gain[:, columns]
                normed[place, columns] = value.astype(BF16)

    gate = jnp.dot(normed[...], gate_weight[0], preferred_element_type=F32)
    up = jnp.dot(normed[...], up_weight[0], preferred_element_type=F32)
    value = gate / (1.0 + jnp.exp(-gate)) * up
    for block, mask in enumerate(masks):
        place = slice(block * rows, (block + 1) * rows)
        source = pl.ds(pl.multiple_of((me_x ^ mask) * rows, rows), rows)
        hidden[step, place, :] = (value[place, :] * gates[0, source, :]).astype(BF16)

    @pl.when(step == pl.num_programs(0) - 1)
    def _():
        fetch.wait()
        every = jnp.concatenate([hidden[one] for one in range(hidden.shape[0])], axis=1)
        for mask in range(count):
            columns = pl.ds(pl.multiple_of((me_y ^ mask) * width, width), width)
            terms = jnp.dot(every, held[:, columns], preferred_element_type=F32).astype(BF16)
            for block in range(blocks):
                (odd if mask % 2 else even)[mask // 2, block] = terms[
                    block * rows : (block + 1) * rows, :
                ]


def per_device(
    tokens,
    attention_gain,
    projection_weight,
    output_weight,
    prompt_cache,
    cache_length,
    prompt_group,
    parents,
    accepted_path,
    expert_gain,
    gate_up_weight,
    down_weight,
    route_experts,
    route_gates,
):
    gx_count, gy_count = lax.axis_size("gx"), lax.axis_size("gy")
    ids = jnp.stack([lax.axis_index("gx"), lax.axis_index("gy")]).astype(jnp.int32)
    rows, width = tokens.shape
    depth = attention_gain.shape[0]
    requests, draft = parents.shape
    groups = prompt_cache.shape[0]
    heads = width // HD

    output_full = lax.all_gather(output_weight, "gx", axis=0, tiled=True)

    wide_tokens = tokens.astype(F32)
    squares = jnp.sum(wide_tokens * wide_tokens, axis=1, keepdims=True)
    for bit in range(gy_count.bit_length() - 1):
        squares = squares + swap(squares, "gy", 1 << bit)
    row_scale = lax.rsqrt(squares / depth + 1e-05)

    share = gy_count // gx_count
    route = [
        (a * gy_count + b, (b // share) * gy_count + a * share + b % share)
        for a in range(gx_count)
        for b in range(gy_count)
    ]
    moved = lax.ppermute(tokens, ("gx", "gy"), route)
    experts = gate_up_weight.shape[0]
    units = gate_up_weight.shape[3]
    expert_ids = lax.axis_index("gy") * experts + jnp.arange(experts, dtype=jnp.int32)
    hit = route_experts[None] == expert_ids[:, None, None]
    gates = jnp.sum(jnp.where(hit, route_gates.astype(F32)[None], 0.0), axis=2)[:, :, None]
    gate_weight, moved = lax.optimization_barrier((gate_up_weight[:, :, 0], moved))
    far = gather_far(moved)
    source, moved = lax.optimization_barrier((gate_up_weight, moved))
    up_weight, gates, far = lax.optimization_barrier((source[:, :, 1], gates, far))
    pieces = gather_near(far)
    types = [F32] + [BF16] * (gx_count - 1)
    projected = pl.pallas_call(
        lambda *refs: project_kernel(gy_count, *refs),
        out_shape=[jax.ShapeDtypeStruct((rows, width), kind) for kind in types]
        + [jax.ShapeDtypeStruct((2, rows, width), kind) for kind in types],
        in_specs=[smem()] + [vmem()] * (2 + gy_count),
        out_specs=[vmem()] * (2 * gx_count),
        scratch_shapes=[pltpu.VMEM((gx_count * rows, share * width), BF16)],
        compiler_params=params(),
        name="project",
    )(
        ids, attention_gain.reshape(1, depth), jnp.transpose(projection_weight, (1, 0, 2)), *pieces
    )
    query_terms, pair_terms = projected[:gx_count], projected[gx_count:]
    query_terms = [query_terms[0]] + [
        swap(query_terms[mask], "gx", mask) for mask in range(1, gx_count)
    ]
    pair_terms = [pair_terms[0]] + [
        swap(pair_terms[mask], "gx", mask) for mask in range(1, gx_count)
    ]

    owner = prompt_group % groups
    order = jnp.arange(requests, dtype=jnp.int32)
    ahead = (owner[None, :] < owner[:, None]) | (
        (owner[None, :] == owner[:, None]) & (order[None, :] < order[:, None])
    )
    place = jnp.sum(ahead.astype(jnp.int32), axis=1)
    group_ids = jnp.arange(groups, dtype=jnp.int32)
    held = jnp.sum((owner[None, :] == group_ids[:, None]).astype(jnp.int32), axis=1)
    first = jnp.sum((owner[None, :] < group_ids[:, None]).astype(jnp.int32), axis=1)

    slots = prompt_cache.shape[2]
    step = min(CACHE_BLOCK, slots)
    wide_rows = heads * draft
    flat = lambda *_: (0, 0)
    top, mass, mixed, query = pl.pallas_call(
        lambda *refs: cache_kernel(requests, draft, heads, gx_count, *refs),
        grid_spec=pltpu.PrefetchScalarGridSpec(
            num_scalar_prefetch=4,
            grid=(groups, slots // step),
            in_specs=[pl.BlockSpec((rows, 1), flat)]
            + [pl.BlockSpec((rows, width), flat)] * gx_count
            + [
                pl.BlockSpec(
                    (1, 2, step, width),
                    lambda group, block, lengths, first, held, place: (
                        group,
                        0,
                        jnp.where(
                            held[group] > 0, jnp.minimum(block, (lengths[group] - 1) // step), 0
                        ),
                        0,
                    ),
                ),
            ],
            out_specs=[
                pl.BlockSpec((requests * wide_rows, HD), flat),
                pl.BlockSpec((requests * wide_rows, HD), flat),
                pl.BlockSpec((requests * wide_rows, width), flat),
                pl.BlockSpec((rows, width), flat),
            ],
            scratch_shapes=[pltpu.VMEM((requests * wide_rows, width), BF16)],
        ),
        out_shape=(
            jax.ShapeDtypeStruct((requests * wide_rows, HD), F32),
            jax.ShapeDtypeStruct((requests * wide_rows, HD), F32),
            jax.ShapeDtypeStruct((requests * wide_rows, width), F32),
            jax.ShapeDtypeStruct((rows, width), BF16),
        ),
        compiler_params=params(),
        cost_estimate=cost(20 * rows * slots * width, 4 * groups * slots * width),
        name="cache",
    )(cache_length, first, held, place, row_scale, *query_terms, prompt_cache)

    accepted = accepted_path.shape[1]
    chosen = (jnp.arange(requests, dtype=jnp.int32)[:, None] * draft + accepted_path).reshape(-1, 1)
    attended, picked = pl.pallas_call(
        lambda *refs: draft_kernel(requests, draft, heads, gx_count, *refs),
        out_shape=(
            jax.ShapeDtypeStruct((rows, width), BF16),
            jax.ShapeDtypeStruct((2, requests * accepted, width), BF16),
        ),
        in_specs=[smem()] + [vmem()] * (gx_count + 7),
        out_specs=(vmem(), vmem()),
        scratch_shapes=[
            pltpu.VMEM((rows, width), BF16),
            pltpu.VMEM((rows, width), BF16),
        ],
        compiler_params=params(),
        name="draft",
    )(place, row_scale, *pair_terms, query, ancestor_table(parents), chosen, top, mass, mixed)
    compacted = jnp.transpose(picked, (1, 0, 2))

    half = jax.ShapeDtypeStruct((gy_count // 2, rows, width), BF16)
    even, odd = pl.pallas_call(
        lambda *refs: output_kernel(gy_count, *refs),
        out_shape=(half, half),
        in_specs=[smem(), vmem(), vmem()],
        out_specs=(vmem(), vmem()),
        compiler_params=params(),
        name="output",
    )(ids, attended, output_full)

    summed = even.astype(F32) + swap(odd, "gy", 1).astype(F32)
    stream = tokens.astype(F32) + summed[0]
    for place in range(1, gy_count // 2):
        stream = stream + swap(summed[place].astype(BF16), "gy", 2 * place).astype(F32)
    stream = stream.astype(BF16)

    units_of = [(one, one + 2) for one in range(gx_count) if not one & 2]
    blocks = [stream] + [swap(stream, "gx", mask) for mask in range(1, gx_count)]
    inputs = [one for turn, mask in enumerate(units_of[0]) for one in double_gy(blocks[mask], turn)]
    result = stream.astype(F32)
    pending, waiting, last = [], [], None
    half = jax.ShapeDtypeStruct((gy_count // 2, 2, rows, width), BF16)
    for number, masks in enumerate(units_of):
        after = []
        if number + 1 < len(units_of):
            after = [jnp.stack([blocks[mask] for mask in units_of[number + 1]])]
        inputs, waiting, after = lax.optimization_barrier((inputs, waiting, after))
        far = [gather_far(one) for one in after]
        arrived = [swap(one, "gy", 2 * place) for place, one in enumerate(waiting) if place]
        odd, even = pl.pallas_call(
            lambda *refs: expert_kernel(gy_count, masks, number > 0, *refs),
            grid=(experts,),
            in_specs=[
                smem(),
                pl.BlockSpec((1, depth), lambda expert: (0, 0)),
                pl.BlockSpec((1, gx_count * rows, 1), lambda expert: (expert, 0, 0)),
                pl.BlockSpec((1, depth, units), lambda expert: (expert, 0, 0)),
                pl.BlockSpec((1, depth, units), lambda expert: (expert, 0, 0)),
                pl.BlockSpec(memory_space=pl.ANY),
            ]
            + [vmem()] * len(inputs),
            out_specs=[vmem(), vmem()],
            out_shape=(half, half),
            scratch_shapes=[
                pltpu.VMEM((2 * rows, depth), BF16),
                pltpu.VMEM((experts, 2 * rows, units), BF16),
                pltpu.VMEM((experts * units, depth), BF16),
                pltpu.SemaphoreType.DMA,
            ],
            compiler_params=params(),
            cost_estimate=cost(12 * rows * depth * experts * units, 6 * depth * experts * units),
            name="experts",
        )(
            ids,
            expert_gain.reshape(1, depth),
            gates,
            gate_weight,
            up_weight,
            down_weight.reshape(experts * units, depth),
            *inputs,
        )
        odd, even, far, arrived = lax.optimization_barrier((odd, even, far, arrived))
        if waiting:
            total = sum([one.astype(F32) for one in arrived], waiting[0])
            pending += list(zip(last, total))
        last = masks
        near = swap(odd, "gy", 1)
        inputs = [one for pieces in far for one in gather_near(pieces)]
        summed = even.astype(F32) + near.astype(F32)
        if after:
            waiting = [summed[0]] + [one.astype(BF16) for one in summed[1:]]
        else:
            pending += [(mask, halve_gy(summed[:, turn], turn)) for turn, mask in enumerate(masks)]
    for mask, total in pending:
        if mask:
            total = swap(total.astype(BF16), "gx", mask).astype(F32)
        result = result + total
    return (result.astype(BF16), compacted)


def gather_far(value):
    return [value] + [swap(value, "gy", mask) for mask in range(2, lax.axis_size("gy"), 2)]


def gather_near(even):
    return [one for held in even for one in (held, swap(held, "gy", 1))]


def gather_gy(value):
    return gather_near(gather_far(value))


def far_bits(turn):
    bits = list(range(1, lax.axis_size("gy").bit_length() - 1))
    return bits[::-1] if turn else bits


def double_gy(value, turn):
    held = {0: value}
    for bit in far_bits(turn):
        held.update({mask | 1 << bit: swap(one, "gy", 1 << bit) for mask, one in held.items()})
    held.update({mask | 1: swap(one, "gy", 1) for mask, one in held.items()})
    return [held[mask] for mask in range(len(held))]


def halve_gy(value, turn):
    held = [(2 * place, value[place]) for place in range(value.shape[0])]
    for bit in far_bits(turn):
        mine = [(mask, one) for mask, one in held if not mask >> bit & 1]
        sent = jnp.stack([one for mask, one in held if mask >> bit & 1]).astype(BF16)
        got = swap(sent, "gy", 1 << bit).astype(F32)
        held = [(mask, one + got[place]) for place, (mask, one) in enumerate(mine)]
    return held[0][1]


def solution(mesh):
    placed = (
        P("gx", "gy"),
        P(),
        P("gx", None, "gy"),
        P("gx", "gy"),
        P("gx", None, None, "gy"),
        P("gx"),
        P("gx"),
        P("gx", None),
        P("gx", None),
        P(),
        P("gy", None, None, "gx"),
        P("gy", "gx", None),
        P(),
        P(),
    )
    return jax.shard_map(
        per_device,
        mesh=mesh,
        in_specs=placed,
        out_specs=(P("gx", "gy"), P("gx", None, "gy")),
        check_vma=False,
    )
```

```python
import math

import jax
import jax.numpy as jnp
from jax import lax
from jax.experimental import pallas as pl
from jax.experimental.pallas import tpu as pltpu
from jax.sharding import PartitionSpec as P

HD = 128
CACHE_BLOCK = 1024
VMEM_LIMIT = 56 * 1024 * 1024
BF16 = jnp.bfloat16
F32 = jnp.float32
EXPONENT = math.log2(math.e) / math.sqrt(HD)


def vmem():
    return pl.BlockSpec(memory_space=pltpu.VMEM)


def smem():
    return pl.BlockSpec(memory_space=pltpu.SMEM)


def params():
    return pltpu.CompilerParams(vmem_limit_bytes=VMEM_LIMIT)


def swap(value, axis, mask):
    count = lax.axis_size(axis)
    return lax.ppermute(value, axis, [(one, one ^ mask) for one in range(count)])


def cost(flops, size):
    return pl.CostEstimate(flops=flops, bytes_accessed=size, transcendentals=0)


def ancestor_table(parents):
    nodes = parents.shape[-1]
    column = jnp.arange(nodes, dtype=jnp.int32)
    reach = (parents[:, :, None] == column[None, None, :]).astype(F32)
    reach = reach + jnp.eye(nodes, dtype=F32)[None]
    for _ in range((nodes - 1).bit_length()):
        reach = jnp.minimum(jnp.einsum("rij,rjk->rik", reach, reach), 1.0)
    return reach


def project_kernel(count, ids, gain, weight, *refs):
    pieces, outs, scaled = refs[:count], refs[count:-1], refs[-1]
    me_x, me_y = ids[0], ids[1]
    rows, width = pieces[0].shape
    share = scaled.shape[1] // width
    for mask, piece in enumerate(pieces):
        source = me_y ^ mask
        block, part = source // share, source % share
        columns = pl.ds(pl.multiple_of((me_x * share + part) * width, width), width)
        value = (piece[...].astype(F32) * gain[:, columns]).astype(BF16)
        scaled[
            pl.ds(pl.multiple_of(block * rows, rows), rows),
            pl.ds(pl.multiple_of(part * width, width), width),
        ] = value
    blocks = len(outs) // 2
    for mask in range(blocks):
        place = pl.ds(pl.multiple_of((me_x ^ mask) * rows, rows), rows)
        for which in range(3):
            value = jnp.dot(scaled[place, :], weight[which], preferred_element_type=F32)
            if which == 0:
                outs[mask][...] = value.astype(outs[mask].dtype)
            else:
                out = outs[blocks + mask]
                out[which - 1] = value.astype(out.dtype)


def blocked_query(query, request, draft, heads):
    rows = query[request * draft : (request + 1) * draft, :]
    if heads == 1:
        return rows
    column = lax.broadcasted_iota(jnp.int32, rows.shape, 1) // HD
    return jnp.concatenate(
        [jnp.where(column == head, rows, jnp.zeros_like(rows)) for head in range(heads)], axis=0
    )


def cache_kernel(
    requests, draft, heads, parts, lengths, first, held, place, scale_of, *refs
):
    terms, (cache, top, mass, mixed, query, wide) = refs[:parts], refs[parts:]
    group, block = pl.program_id(0), pl.program_id(1)
    slots = cache.shape[2]
    size = heads * draft

    @pl.when((group == 0) & (block == 0))
    def _():
        top[...] = jnp.full(top.shape, -jnp.inf, F32)
        mass[...] = jnp.zeros(mass.shape, F32)
        mixed[...] = jnp.zeros(mixed.shape, F32)
        total = terms[0][...]
        for term in terms[1:]:
            total = total + term[...].astype(F32)
        query[...] = (total * scale_of[...]).astype(BF16)
        for request in range(requests):
            rows = pl.ds(pl.multiple_of(place[request] * size, size), size)
            wide[rows, :] = blocked_query(query[...], request, draft, heads)

    left = lengths[group] - block * slots
    for count in range(1, requests + 1):

        @pl.when((held[group] == count) & (left > 0))
        def _():
            rows = pl.ds(pl.multiple_of(first[group] * size, size), count * size)
            scores = lax.dot_general(
                wide[rows, :],
                cache[0, 0],
                (((1,), (1,)), ((), ())),
                preferred_element_type=F32,
            )
            column = lax.broadcasted_iota(jnp.int32, (1, slots), 1)
            scores = scores + jnp.where(column < left, 0.0, -jnp.inf)
            before = top[rows, :]
            now = jnp.maximum(before, jnp.max(scores, axis=1, keepdims=True))
            spread = jnp.concatenate([now] * (slots // now.shape[1]), axis=1)
            powered = jnp.exp2((scores - spread) * EXPONENT)
            fade = jnp.exp2((before - now) * EXPONENT)
            top[rows, :] = now
            mass[rows, :] = mass[rows, :] * fade + jnp.sum(powered, axis=1, keepdims=True)
            mixed[rows, :] = mixed[rows, :] * jnp.concatenate([fade] * heads, axis=1) + jnp.dot(
                powered.astype(BF16), cache[0, 1], preferred_element_type=F32
            )


def draft_kernel(requests, draft, heads, parts, place, scale_of, *refs):
    pairs = refs[:parts]
    query, reach, rows, top, mass, mixed, attended, picked, key, value = refs[parts:]
    for which, kept in ((0, key), (1, value)):
        total = pairs[0][which]
        for pair in pairs[1:]:
            total = total + pair[which].astype(F32)
        kept[...] = (total * scale_of[...]).astype(BF16)
    tokens = key.shape[0]
    chosen = (
        lax.broadcasted_iota(jnp.int32, (rows.shape[0], tokens), 1) == rows[...]
    ).astype(BF16)
    picked[0] = jnp.dot(chosen, key[...], preferred_element_type=F32).astype(BF16)
    picked[1] = jnp.dot(chosen, value[...], preferred_element_type=F32).astype(BF16)
    size = heads * draft
    for request in range(requests):
        own = slice(request * draft, (request + 1) * draft)
        kept = pl.ds(pl.multiple_of(place[request] * size, size), size)
        wide = blocked_query(query[...], request, draft, heads)
        scores = lax.dot_general(
            wide, key[own, :], (((1,), (1,)), ((), ())), preferred_element_type=F32
        )
        seen = jnp.concatenate([reach[request]] * heads, axis=0)
        scores = jnp.where(seen > 0, scores, -jnp.inf)
        before = top[kept, :][:, :1]
        now = jnp.maximum(before, jnp.max(scores, axis=1, keepdims=True))
        powered = jnp.exp2((scores - now) * EXPONENT)
        fade = jnp.exp2((before - now) * EXPONENT)
        sums = mass[kept, :][:, :1] * fade + jnp.sum(powered, axis=1, keepdims=True)
        total = mixed[kept, :] * fade + jnp.dot(
            powered.astype(BF16), value[own, :], preferred_element_type=F32
        )
        total = (total / sums).astype(BF16)
        for head in range(heads):
            attended[own, head * HD : (head + 1) * HD] = total[
                head * draft : (head + 1) * draft, head * HD : (head + 1) * HD
            ]


def output_kernel(count, ids, attended, output, *outs):
    me = ids[1]
    rows, width = outs[0].shape[-2:]
    for mask in range(count):
        place = pl.ds(pl.multiple_of((me ^ mask) * width, width), width)
        value = lax.dot_general(
            attended[...],
            output[place, :],
            (((1,), (1,)), ((), ())),
            preferred_element_type=F32,
        ).astype(BF16)
        outs[mask % 2][mask // 2] = value


def expert_kernel(count, masks, stacked, ids, gain, route, route_gate, weight, down, *refs):
    blocks = len(masks)
    pieces, (odd, even, normed, hidden, held, arrival) = refs[:-6], refs[-6:]
    me_x, me_y = ids[0], ids[1]
    rows, width = pieces[0].shape[-2:]
    step = pl.program_id(0)
    fetch = pltpu.make_async_copy(down, held, arrival)

    @pl.when(step == 0)
    def _():
        fetch.start()
        for block in range(blocks):
            if stacked:
                own = [piece.at[block] for piece in pieces]
            else:
                own = pieces[block * count : (block + 1) * count]
            place = slice(block * rows, (block + 1) * rows)
            squares = jnp.zeros((rows, 1), F32)
            for piece in own:
                value = piece[...].astype(F32)
                squares = squares + jnp.sum(value * value, axis=1, keepdims=True)
            scale = lax.rsqrt(squares / (width * count) + 1e-05)
            for mask, piece in enumerate(own):
                columns = pl.ds(pl.multiple_of((me_y ^ mask) * width, width), width)
                value = piece[...].astype(F32) * scale * gain[:, columns]
                normed[place, columns] = value.astype(BF16)

    gate = jnp.dot(normed[...], weight[0, 0], preferred_element_type=F32)
    up = jnp.dot(normed[...], weight[1, 0], preferred_element_type=F32)
    expert = me_y * pl.num_programs(0) + step
    value = gate / (1.0 + jnp.exp(-gate)) * up
    for block, mask in enumerate(masks):
        place = slice(block * rows, (block + 1) * rows)
        source = pl.ds(pl.multiple_of((me_x ^ mask) * rows, rows), rows)
        chosen = jnp.where(route[:, source] == expert, route_gate[:, source], 0.0)
        factor = lax.dot_general(
            chosen.astype(BF16),
            jnp.ones((chosen.shape[0], value.shape[1]), BF16),
            (((0,), (0,)), ((), ())),
            preferred_element_type=F32,
        )
        hidden[step, place, :] = (value[place, :] * factor).astype(BF16)

    @pl.when(step == pl.num_programs(0) - 1)
    def _():
        fetch.wait()
        every = jnp.concatenate([hidden[one] for one in range(hidden.shape[0])], axis=1)
        for mask in range(count):
            columns = pl.ds(pl.multiple_of((me_y ^ mask) * width, width), width)
            terms = jnp.dot(every, held[:, columns], preferred_element_type=F32).astype(BF16)
            for block in range(blocks):
                (odd if mask % 2 else even)[mask // 2, block] = terms[
                    block * rows : (block + 1) * rows, :
                ]


def per_device(
    tokens,
    attention_gain,
    projection_weight,
    output_weight,
    prompt_cache,
    cache_length,
    prompt_group,
    parents,
    accepted_path,
    expert_gain,
    gate_up_weight,
    down_weight,
    route_experts,
    route_gates,
):
    gx_count, gy_count = lax.axis_size("gx"), lax.axis_size("gy")
    ids = jnp.stack([lax.axis_index("gx"), lax.axis_index("gy")]).astype(jnp.int32)
    rows, width = tokens.shape
    depth = attention_gain.shape[0]
    requests, draft = parents.shape
    groups = prompt_cache.shape[0]
    heads = width // HD

    wide_tokens = tokens.astype(F32)
    squares = jnp.sum(wide_tokens * wide_tokens, axis=1, keepdims=True)
    for bit in range(gy_count.bit_length() - 1):
        squares = squares + swap(squares, "gy", 1 << bit)
    row_scale = lax.rsqrt(squares / depth + 1e-05)

    share = gy_count // gx_count
    route = [
        (a * gy_count + b, (b // share) * gy_count + a * share + b % share)
        for a in range(gx_count)
        for b in range(gy_count)
    ]
    moved = lax.ppermute(tokens, ("gx", "gy"), route)
    experts = gate_up_weight.shape[0]
    units = gate_up_weight.shape[3]
    output_full = lax.all_gather(output_weight, "gx", axis=0, tiled=True)
    far = gather_far(moved)
    gate_up, far = lax.optimization_barrier((jnp.transpose(gate_up_weight, (2, 0, 1, 3)), far))
    pieces = gather_near(far)
    types = [F32] + [BF16] * (gx_count - 1)
    projected = pl.pallas_call(
        lambda *refs: project_kernel(gy_count, *refs),
        out_shape=[jax.ShapeDtypeStruct((rows, width), kind) for kind in types]
        + [jax.ShapeDtypeStruct((2, rows, width), kind) for kind in types],
        in_specs=[smem()] + [vmem()] * (2 + gy_count),
        out_specs=[vmem()] * (2 * gx_count),
        scratch_shapes=[pltpu.VMEM((gx_count * rows, share * width), BF16)],
        compiler_params=params(),
        name="project",
    )(
        ids, attention_gain.reshape(1, depth), jnp.transpose(projection_weight, (1, 0, 2)), *pieces
    )
    query_terms, pair_terms = projected[:gx_count], projected[gx_count:]
    parents, query_terms = lax.optimization_barrier((parents, query_terms))
    query_terms = [query_terms[0]] + [
        swap(query_terms[mask], "gx", mask) for mask in range(1, gx_count)
    ]
    pair_terms = [pair_terms[0]] + [
        swap(pair_terms[mask], "gx", mask) for mask in range(1, gx_count)
    ]

    owner = prompt_group % groups
    order = jnp.arange(requests, dtype=jnp.int32)
    ahead = (owner[None, :] < owner[:, None]) | (
        (owner[None, :] == owner[:, None]) & (order[None, :] < order[:, None])
    )
    place = jnp.sum(ahead.astype(jnp.int32), axis=1)
    group_ids = jnp.arange(groups, dtype=jnp.int32)
    held = jnp.sum((owner[None, :] == group_ids[:, None]).astype(jnp.int32), axis=1)
    first = jnp.sum((owner[None, :] < group_ids[:, None]).astype(jnp.int32), axis=1)

    slots = prompt_cache.shape[2]
    step = min(CACHE_BLOCK, slots)
    wide_rows = heads * draft
    flat = lambda *_: (0, 0)
    top, mass, mixed, query = pl.pallas_call(
        lambda *refs: cache_kernel(requests, draft, heads, gx_count, *refs),
        grid_spec=pltpu.PrefetchScalarGridSpec(
            num_scalar_prefetch=4,
            grid=(groups, slots // step),
            in_specs=[pl.BlockSpec((rows, 1), flat)]
            + [pl.BlockSpec((rows, width), flat)] * gx_count
            + [
                pl.BlockSpec(
                    (1, 2, step, width),
                    lambda group, block, lengths, first, held, place: (
                        group,
                        0,
                        jnp.where(
                            held[group] > 0, jnp.minimum(block, (lengths[group] - 1) // step), 0
                        ),
                        0,
                    ),
                ),
            ],
            out_specs=[
                pl.BlockSpec((requests * wide_rows, HD), flat),
                pl.BlockSpec((requests * wide_rows, HD), flat),
                pl.BlockSpec((requests * wide_rows, width), flat),
                pl.BlockSpec((rows, width), flat),
            ],
            scratch_shapes=[pltpu.VMEM((requests * wide_rows, width), BF16)],
        ),
        out_shape=(
            jax.ShapeDtypeStruct((requests * wide_rows, HD), F32),
            jax.ShapeDtypeStruct((requests * wide_rows, HD), F32),
            jax.ShapeDtypeStruct((requests * wide_rows, width), F32),
            jax.ShapeDtypeStruct((rows, width), BF16),
        ),
        compiler_params=params(),
        cost_estimate=cost(20 * rows * slots * width, 4 * groups * slots * width),
        name="cache",
    )(cache_length, first, held, place, row_scale, *query_terms, prompt_cache)

    accepted = accepted_path.shape[1]
    chosen = (jnp.arange(requests, dtype=jnp.int32)[:, None] * draft + accepted_path).reshape(-1, 1)
    attended, picked = pl.pallas_call(
        lambda *refs: draft_kernel(requests, draft, heads, gx_count, *refs),
        out_shape=(
            jax.ShapeDtypeStruct((rows, width), BF16),
            jax.ShapeDtypeStruct((2, requests * accepted, width), BF16),
        ),
        in_specs=[smem()] + [vmem()] * (gx_count + 7),
        out_specs=(vmem(), vmem()),
        scratch_shapes=[
            pltpu.VMEM((rows, width), BF16),
            pltpu.VMEM((rows, width), BF16),
        ],
        compiler_params=params(),
        name="draft",
    )(place, row_scale, *pair_terms, query, ancestor_table(parents), chosen, top, mass, mixed)
    compacted = jnp.transpose(picked, (1, 0, 2))

    half = jax.ShapeDtypeStruct((gy_count // 2, rows, width), BF16)
    even, odd = pl.pallas_call(
        lambda *refs: output_kernel(gy_count, *refs),
        out_shape=(half, half),
        in_specs=[smem(), vmem(), vmem()],
        out_specs=(vmem(), vmem()),
        compiler_params=params(),
        name="output",
    )(ids, attended, output_full)

    summed = even.astype(F32) + swap(odd, "gy", 1).astype(F32)
    stream = tokens.astype(F32) + summed[0]
    for place in range(1, gy_count // 2):
        stream = stream + swap(summed[place].astype(BF16), "gy", 2 * place).astype(F32)
    stream = stream.astype(BF16)

    units_of = [(one, one + 2) for one in range(gx_count) if not one & 2]
    blocks = [stream] + [swap(stream, "gx", mask) for mask in range(1, gx_count)]
    inputs = [one for turn, mask in enumerate(units_of[0]) for one in double_gy(blocks[mask], turn)]
    result = stream.astype(F32)
    waiting, last = [], None
    half = jax.ShapeDtypeStruct((gy_count // 2, 2, rows, width), BF16)
    for number, masks in enumerate(units_of):
        after = []
        if number + 1 < len(units_of):
            after = [jnp.stack([blocks[mask] for mask in units_of[number + 1]])]
        inputs, waiting, after = lax.optimization_barrier((inputs, waiting, after))
        far = [gather_far(one) for one in after]
        arrived = [swap(one, "gy", 2 * place) for place, one in enumerate(waiting) if place]
        odd, even = pl.pallas_call(
            lambda *refs: expert_kernel(gy_count, masks, number > 0, *refs),
            grid=(experts,),
            in_specs=[
                smem(),
                pl.BlockSpec((1, depth), lambda expert: (0, 0)),
                vmem(),
                vmem(),
                pl.BlockSpec((2, 1, depth, units), lambda expert: (0, expert, 0, 0)),
                pl.BlockSpec(memory_space=pl.ANY),
            ]
            + [vmem()] * len(inputs),
            out_specs=[vmem(), vmem()],
            out_shape=(half, half),
            scratch_shapes=[
                pltpu.VMEM((2 * rows, depth), BF16),
                pltpu.VMEM((experts, 2 * rows, units), BF16),
                pltpu.VMEM((experts * units, depth), BF16),
                pltpu.SemaphoreType.DMA,
            ],
            compiler_params=params(),
            cost_estimate=cost(12 * rows * depth * experts * units, 6 * depth * experts * units),
            name="experts",
        )(
            ids,
            expert_gain.reshape(1, depth),
            route_experts.T,
            route_gates.astype(F32).T,
            gate_up,
            down_weight.reshape(experts * units, depth),
            *inputs,
        )
        odd, even, far, arrived = lax.optimization_barrier((odd, even, far, arrived))
        if waiting:
            total = sum([one.astype(F32) for one in arrived], waiting[0])
            for mask, one in zip(last, total):
                if mask:
                    one = swap(one.astype(BF16), "gx", mask).astype(F32)
                result = result + one
        last = masks
        near = swap(odd, "gy", 1)
        inputs = [one for pieces in far for one in gather_near(pieces)]
        summed = even.astype(F32) + near.astype(F32)
        if after:
            waiting = [summed[0]] + [one.astype(BF16) for one in summed[1:]]
        else:
            totals, result = halve_gy([summed[:, turn] for turn in range(len(masks))], result)
    for mask, one in zip(masks, totals):
        if mask:
            one = swap(one.astype(BF16), "gx", mask).astype(F32)
        result = result + one
    return (result.astype(BF16), compacted)


def gather_far(value):
    return [value] + [swap(value, "gy", mask) for mask in range(2, lax.axis_size("gy"), 2)]


def gather_near(even):
    return [one for held in even for one in (held, swap(held, "gy", 1))]


def gather_gy(value):
    return gather_near(gather_far(value))


def far_bits(turn):
    bits = list(range(1, lax.axis_size("gy").bit_length() - 1))
    return bits[::-1] if turn else bits


def double_gy(value, turn):
    held = {0: value}
    for bit in far_bits(turn):
        held.update({mask | 1 << bit: swap(one, "gy", 1 << bit) for mask, one in held.items()})
    held.update({mask | 1: swap(one, "gy", 1) for mask, one in held.items()})
    return [held[mask] for mask in range(len(held))]


def halve_gy(values, early):
    many = [[(2 * place, value[place]) for place in range(value.shape[0])] for value in values]
    orders = [far_bits(turn % 2) for turn in range(len(values))]
    for step in range(len(orders[0])):
        sent = [
            jnp.stack([one for mask, one in held if mask >> order[step] & 1]).astype(BF16)
            for held, order in zip(many, orders)
        ]
        if step + 1 == len(orders[0]):
            sent, early = lax.optimization_barrier((sent, early))
        for turn, order in enumerate(orders):
            got = swap(sent[turn], "gy", 1 << order[step]).astype(F32)
            mine = [(mask, one) for mask, one in many[turn] if not mask >> order[step] & 1]
            many[turn] = [(mask, one + got[place]) for place, (mask, one) in enumerate(mine)]
    return [held[0][1] for held in many], early


def solution(mesh):
    placed = (
        P("gx", "gy"),
        P(),
        P("gx", None, "gy"),
        P("gx", "gy"),
        P("gx", None, None, "gy"),
        P("gx"),
        P("gx"),
        P("gx", None),
        P("gx", None),
        P(),
        P("gy", None, None, "gx"),
        P("gy", "gx", None),
        P(),
        P(),
    )
    return jax.shard_map(
        per_device,
        mesh=mesh,
        in_specs=placed,
        out_specs=(P("gx", "gy"), P("gx", None, "gy")),
        check_vma=False,
    )
```

```python
import math

import jax
import jax.numpy as jnp
from jax import lax
from jax.experimental import pallas as pl
from jax.experimental.pallas import tpu as pltpu
from jax.sharding import PartitionSpec as P

HD = 128
CACHE_BLOCK = 1024
VMEM_LIMIT = 56 * 1024 * 1024
BF16 = jnp.bfloat16
F32 = jnp.float32
EXPONENT = math.log2(math.e) / math.sqrt(HD)


def vmem():
    return pl.BlockSpec(memory_space=pltpu.VMEM)


def smem():
    return pl.BlockSpec(memory_space=pltpu.SMEM)


def params():
    return pltpu.CompilerParams(vmem_limit_bytes=VMEM_LIMIT)


def swap(value, axis, mask):
    count = lax.axis_size(axis)
    return lax.ppermute(value, axis, [(one, one ^ mask) for one in range(count)])


def cost(flops, size):
    return pl.CostEstimate(flops=flops, bytes_accessed=size, transcendentals=0)


def ancestor_table(parents):
    nodes = parents.shape[-1]
    column = jnp.arange(nodes, dtype=jnp.int32)
    reach = (parents[:, :, None] == column[None, None, :]).astype(F32)
    reach = reach + jnp.eye(nodes, dtype=F32)[None]
    for _ in range((nodes - 1).bit_length()):
        reach = jnp.minimum(jnp.einsum("rij,rjk->rik", reach, reach), 1.0)
    return reach


def project_kernel(count, ids, gain, weight, *refs):
    pieces, outs, scaled = refs[:count], refs[count:-1], refs[-1]
    me_x, me_y = ids[0], ids[1]
    rows, width = pieces[0].shape
    share = scaled.shape[1] // width
    for mask, piece in enumerate(pieces):
        source = me_y ^ mask
        block, part = source // share, source % share
        columns = pl.ds(pl.multiple_of((me_x * share + part) * width, width), width)
        value = (piece[...].astype(F32) * gain[:, columns]).astype(BF16)
        scaled[
            pl.ds(pl.multiple_of(block * rows, rows), rows),
            pl.ds(pl.multiple_of(part * width, width), width),
        ] = value
    blocks = len(outs) // 2
    for mask in range(blocks):
        place = pl.ds(pl.multiple_of((me_x ^ mask) * rows, rows), rows)
        for which in range(3):
            value = jnp.dot(scaled[place, :], weight[which], preferred_element_type=F32)
            if which == 0:
                outs[mask][...] = value.astype(outs[mask].dtype)
            else:
                out = outs[blocks + mask]
                out[which - 1] = value.astype(out.dtype)


def blocked_query(query, request, draft, heads):
    rows = query[request * draft : (request + 1) * draft, :]
    if heads == 1:
        return rows
    column = lax.broadcasted_iota(jnp.int32, rows.shape, 1) // HD
    return jnp.concatenate(
        [jnp.where(column == head, rows, jnp.zeros_like(rows)) for head in range(heads)], axis=0
    )


def cache_kernel(
    requests, draft, heads, parts, lengths, first, held, place, scale_of, *refs
):
    terms, (cache, top, mass, mixed, query, wide) = refs[:parts], refs[parts:]
    group, block = pl.program_id(0), pl.program_id(1)
    slots = cache.shape[2]
    size = heads * draft

    @pl.when((group == 0) & (block == 0))
    def _():
        top[...] = jnp.full(top.shape, -jnp.inf, F32)
        mass[...] = jnp.zeros(mass.shape, F32)
        mixed[...] = jnp.zeros(mixed.shape, F32)
        total = terms[0][...]
        for term in terms[1:]:
            total = total + term[...].astype(F32)
        query[...] = (total * scale_of[...]).astype(BF16)
        for request in range(requests):
            rows = pl.ds(pl.multiple_of(place[request] * size, size), size)
            wide[rows, :] = blocked_query(query[...], request, draft, heads)

    left = lengths[group] - block * slots
    for count in range(1, requests + 1):

        @pl.when((held[group] == count) & (left > 0))
        def _():
            rows = pl.ds(pl.multiple_of(first[group] * size, size), count * size)
            scores = lax.dot_general(
                wide[rows, :],
                cache[0, 0],
                (((1,), (1,)), ((), ())),
                preferred_element_type=F32,
            )
            column = lax.broadcasted_iota(jnp.int32, (1, slots), 1)
            scores = scores + jnp.where(column < left, 0.0, -jnp.inf)
            before = top[rows, :]
            now = jnp.maximum(before, jnp.max(scores, axis=1, keepdims=True))
            spread = jnp.concatenate([now] * (slots // now.shape[1]), axis=1)
            powered = jnp.exp2((scores - spread) * EXPONENT)
            fade = jnp.exp2((before - now) * EXPONENT)
            top[rows, :] = now
            mass[rows, :] = mass[rows, :] * fade + jnp.sum(powered, axis=1, keepdims=True)
            mixed[rows, :] = mixed[rows, :] * jnp.concatenate([fade] * heads, axis=1) + jnp.dot(
                powered.astype(BF16), cache[0, 1], preferred_element_type=F32
            )


def draft_kernel(requests, draft, heads, parts, count, ids, place, scale_of, *refs):
    pairs = refs[:parts]
    query, reach, rows, top, mass, mixed, output = refs[parts : parts + 7]
    even, odd, picked, key, value, attended = refs[parts + 7 :]
    me = ids[1]
    for which, kept in ((0, key), (1, value)):
        total = pairs[0][which]
        for pair in pairs[1:]:
            total = total + pair[which].astype(F32)
        kept[...] = (total * scale_of[...]).astype(BF16)
    tokens = key.shape[0]
    chosen = (
        lax.broadcasted_iota(jnp.int32, (rows.shape[0], tokens), 1) == rows[...]
    ).astype(BF16)
    picked[0] = jnp.dot(chosen, key[...], preferred_element_type=F32).astype(BF16)
    picked[1] = jnp.dot(chosen, value[...], preferred_element_type=F32).astype(BF16)
    size = heads * draft
    for request in range(requests):
        own = slice(request * draft, (request + 1) * draft)
        kept = pl.ds(pl.multiple_of(place[request] * size, size), size)
        wide = blocked_query(query[...], request, draft, heads)
        scores = lax.dot_general(
            wide, key[own, :], (((1,), (1,)), ((), ())), preferred_element_type=F32
        )
        seen = jnp.concatenate([reach[request]] * heads, axis=0)
        scores = jnp.where(seen > 0, scores, -jnp.inf)
        before = top[kept, :][:, :1]
        now = jnp.maximum(before, jnp.max(scores, axis=1, keepdims=True))
        powered = jnp.exp2((scores - now) * EXPONENT)
        fade = jnp.exp2((before - now) * EXPONENT)
        sums = mass[kept, :][:, :1] * fade + jnp.sum(powered, axis=1, keepdims=True)
        total = mixed[kept, :] * fade + jnp.dot(
            powered.astype(BF16), value[own, :], preferred_element_type=F32
        )
        total = (total / sums).astype(BF16)
        for head in range(heads):
            attended[own, head * HD : (head + 1) * HD] = total[
                head * draft : (head + 1) * draft, head * HD : (head + 1) * HD
            ]
    width = even.shape[-1]
    for mask in range(count):
        columns = pl.ds(pl.multiple_of((me ^ mask) * width, width), width)
        value = lax.dot_general(
            attended[...],
            output[columns, :],
            (((1,), (1,)), ((), ())),
            preferred_element_type=F32,
        ).astype(BF16)
        (odd if mask % 2 else even)[mask // 2] = value


def expert_kernel(count, masks, stacked, ids, gain, route, route_gate, weight, down, *refs):
    blocks = len(masks)
    pieces, (odd, even, normed, hidden, held, arrival) = refs[:-6], refs[-6:]
    me_x, me_y = ids[0], ids[1]
    rows, width = pieces[0].shape[-2:]
    step = pl.program_id(0)
    fetch = pltpu.make_async_copy(down, held, arrival)

    @pl.when(step == 0)
    def _():
        fetch.start()
        for block in range(blocks):
            if stacked:
                own = [piece.at[block] for piece in pieces]
            else:
                own = pieces[block * count : (block + 1) * count]
            place = slice(block * rows, (block + 1) * rows)
            squares = jnp.zeros((rows, 1), F32)
            for piece in own:
                value = piece[...].astype(F32)
                squares = squares + jnp.sum(value * value, axis=1, keepdims=True)
            scale = lax.rsqrt(squares / (width * count) + 1e-05)
            for mask, piece in enumerate(own):
                columns = pl.ds(pl.multiple_of((me_y ^ mask) * width, width), width)
                value = piece[...].astype(F32) * scale * gain[:, columns]
                normed[place, columns] = value.astype(BF16)

    gate = jnp.dot(normed[...], weight[0, 0], preferred_element_type=F32)
    up = jnp.dot(normed[...], weight[1, 0], preferred_element_type=F32)
    expert = me_y * pl.num_programs(0) + step
    value = gate / (1.0 + jnp.exp(-gate)) * up
    for block, mask in enumerate(masks):
        place = slice(block * rows, (block + 1) * rows)
        source = pl.ds(pl.multiple_of((me_x ^ mask) * rows, rows), rows)
        chosen = jnp.where(route[:, source] == expert, route_gate[:, source], 0.0)
        factor = lax.dot_general(
            chosen.astype(BF16),
            jnp.ones((chosen.shape[0], value.shape[1]), BF16),
            (((0,), (0,)), ((), ())),
            preferred_element_type=F32,
        )
        hidden[step, place, :] = (value[place, :] * factor).astype(BF16)

    @pl.when(step == pl.num_programs(0) - 1)
    def _():
        fetch.wait()
        every = jnp.concatenate([hidden[one] for one in range(hidden.shape[0])], axis=1)
        for mask in range(count):
            columns = pl.ds(pl.multiple_of((me_y ^ mask) * width, width), width)
            terms = jnp.dot(every, held[:, columns], preferred_element_type=F32).astype(BF16)
            for block in range(blocks):
                (odd if mask % 2 else even)[mask // 2, block] = terms[
                    block * rows : (block + 1) * rows, :
                ]


def per_device(
    tokens,
    attention_gain,
    projection_weight,
    output_weight,
    prompt_cache,
    cache_length,
    prompt_group,
    parents,
    accepted_path,
    expert_gain,
    gate_up_weight,
    down_weight,
    route_experts,
    route_gates,
):
    gx_count, gy_count = lax.axis_size("gx"), lax.axis_size("gy")
    ids = jnp.stack([lax.axis_index("gx"), lax.axis_index("gy")]).astype(jnp.int32)
    rows, width = tokens.shape
    depth = attention_gain.shape[0]
    requests, draft = parents.shape
    groups = prompt_cache.shape[0]
    heads = width // HD

    wide_tokens = tokens.astype(F32)
    squares = jnp.sum(wide_tokens * wide_tokens, axis=1, keepdims=True)
    for bit in range(gy_count.bit_length() - 1):
        squares = squares + swap(squares, "gy", 1 << bit)
    row_scale = lax.rsqrt(squares / depth + 1e-05)

    share = gy_count // gx_count
    route = [
        (a * gy_count + b, (b // share) * gy_count + a * share + b % share)
        for a in range(gx_count)
        for b in range(gy_count)
    ]
    moved = lax.ppermute(tokens, ("gx", "gy"), route)
    experts = gate_up_weight.shape[0]
    units = gate_up_weight.shape[3]
    output_full = lax.all_gather(output_weight, "gx", axis=0, tiled=True)
    far = gather_far(moved)
    gate_up, far = lax.optimization_barrier((jnp.transpose(gate_up_weight, (2, 0, 1, 3)), far))
    pieces = gather_near(far)
    types = [F32] + [BF16] * (gx_count - 1)
    projected = pl.pallas_call(
        lambda *refs: project_kernel(gy_count, *refs),
        out_shape=[jax.ShapeDtypeStruct((rows, width), kind) for kind in types]
        + [jax.ShapeDtypeStruct((2, rows, width), kind) for kind in types],
        in_specs=[smem()] + [vmem()] * (2 + gy_count),
        out_specs=[vmem()] * (2 * gx_count),
        scratch_shapes=[pltpu.VMEM((gx_count * rows, share * width), BF16)],
        compiler_params=params(),
        name="project",
    )(
        ids, attention_gain.reshape(1, depth), jnp.transpose(projection_weight, (1, 0, 2)), *pieces
    )
    query_terms, pair_terms = projected[:gx_count], projected[gx_count:]
    parents, query_terms = lax.optimization_barrier((parents, query_terms))
    query_terms = [query_terms[0]] + [
        swap(query_terms[mask], "gx", mask) for mask in range(1, gx_count)
    ]
    pair_terms = [pair_terms[0]] + [
        swap(pair_terms[mask], "gx", mask) for mask in range(1, gx_count)
    ]

    owner = prompt_group % groups
    order = jnp.arange(requests, dtype=jnp.int32)
    ahead = (owner[None, :] < owner[:, None]) | (
        (owner[None, :] == owner[:, None]) & (order[None, :] < order[:, None])
    )
    place = jnp.sum(ahead.astype(jnp.int32), axis=1)
    group_ids = jnp.arange(groups, dtype=jnp.int32)
    held = jnp.sum((owner[None, :] == group_ids[:, None]).astype(jnp.int32), axis=1)
    first = jnp.sum((owner[None, :] < group_ids[:, None]).astype(jnp.int32), axis=1)

    slots = prompt_cache.shape[2]
    step = min(CACHE_BLOCK, slots)
    wide_rows = heads * draft
    flat = lambda *_: (0, 0)
    top, mass, mixed, query = pl.pallas_call(
        lambda *refs: cache_kernel(requests, draft, heads, gx_count, *refs),
        grid_spec=pltpu.PrefetchScalarGridSpec(
            num_scalar_prefetch=4,
            grid=(groups, slots // step),
            in_specs=[pl.BlockSpec((rows, 1), flat)]
            + [pl.BlockSpec((rows, width), flat)] * gx_count
            + [
                pl.BlockSpec(
                    (1, 2, step, width),
                    lambda group, block, lengths, first, held, place: (
                        group,
                        0,
                        jnp.where(
                            held[group] > 0, jnp.minimum(block, (lengths[group] - 1) // step), 0
                        ),
                        0,
                    ),
                ),
            ],
            out_specs=[
                pl.BlockSpec((requests * wide_rows, HD), flat),
                pl.BlockSpec((requests * wide_rows, HD), flat),
                pl.BlockSpec((requests * wide_rows, width), flat),
                pl.BlockSpec((rows, width), flat),
            ],
            scratch_shapes=[pltpu.VMEM((requests * wide_rows, width), BF16)],
        ),
        out_shape=(
            jax.ShapeDtypeStruct((requests * wide_rows, HD), F32),
            jax.ShapeDtypeStruct((requests * wide_rows, HD), F32),
            jax.ShapeDtypeStruct((requests * wide_rows, width), F32),
            jax.ShapeDtypeStruct((rows, width), BF16),
        ),
        compiler_params=params(),
        cost_estimate=cost(20 * rows * slots * width, 4 * groups * slots * width),
        name="cache",
    )(cache_length, first, held, place, row_scale, *query_terms, prompt_cache)

    accepted = accepted_path.shape[1]
    chosen = (jnp.arange(requests, dtype=jnp.int32)[:, None] * draft + accepted_path).reshape(-1, 1)
    half = jax.ShapeDtypeStruct((gy_count // 2, rows, width), BF16)
    even, odd, picked = pl.pallas_call(
        lambda *refs: draft_kernel(requests, draft, heads, gx_count, gy_count, *refs),
        out_shape=(
            half,
            half,
            jax.ShapeDtypeStruct((2, requests * accepted, width), BF16),
        ),
        in_specs=[smem(), smem()] + [vmem()] * (gx_count + 8),
        out_specs=(vmem(), vmem(), vmem()),
        scratch_shapes=[pltpu.VMEM((rows, width), BF16)] * 3,
        compiler_params=params(),
        name="draft",
    )(
        ids,
        place,
        row_scale,
        *pair_terms,
        query,
        ancestor_table(parents),
        chosen,
        top,
        mass,
        mixed,
        output_full,
    )
    compacted = jnp.transpose(picked, (1, 0, 2))

    summed = even.astype(F32) + swap(odd, "gy", 1).astype(F32)
    stream = tokens.astype(F32) + summed[0]
    for place in range(1, gy_count // 2):
        stream = stream + swap(summed[place].astype(BF16), "gy", 2 * place).astype(F32)
    stream = stream.astype(BF16)

    units_of = [(one, one + 2) for one in range(gx_count) if not one & 2]
    blocks = {0: stream, units_of[0][1]: swap(stream, "gx", units_of[0][1])}
    later, blocks[units_of[0][1]] = lax.optimization_barrier((stream, blocks[units_of[0][1]]))
    for mask in range(gx_count):
        if mask not in blocks:
            blocks[mask] = swap(later, "gx", mask)
    inputs = [one for mask in units_of[0] for one in gather_gy(blocks[mask])]
    result = stream.astype(F32)
    waiting, last = [], None
    half = jax.ShapeDtypeStruct((gy_count // 2, 2, rows, width), BF16)
    for number, masks in enumerate(units_of):
        after = []
        if number + 1 < len(units_of):
            after = [jnp.stack([blocks[mask] for mask in units_of[number + 1]])]
        inputs, waiting, after = lax.optimization_barrier((inputs, waiting, after))
        far = [gather_far(one) for one in after]
        arrived = [swap(one, "gy", 2 * place) for place, one in enumerate(waiting) if place]
        odd, even = pl.pallas_call(
            lambda *refs: expert_kernel(gy_count, masks, number > 0, *refs),
            grid=(experts,),
            in_specs=[
                smem(),
                pl.BlockSpec((1, depth), lambda expert: (0, 0)),
                vmem(),
                vmem(),
                pl.BlockSpec((2, 1, depth, units), lambda expert: (0, expert, 0, 0)),
                pl.BlockSpec(memory_space=pl.ANY),
            ]
            + [vmem()] * len(inputs),
            out_specs=[vmem(), vmem()],
            out_shape=(half, half),
            scratch_shapes=[
                pltpu.VMEM((2 * rows, depth), BF16),
                pltpu.VMEM((experts, 2 * rows, units), BF16),
                pltpu.VMEM((experts * units, depth), BF16),
                pltpu.SemaphoreType.DMA,
            ],
            compiler_params=params(),
            cost_estimate=cost(12 * rows * depth * experts * units, 6 * depth * experts * units),
            name="experts",
        )(
            ids,
            expert_gain.reshape(1, depth),
            route_experts.T,
            route_gates.astype(F32).T,
            gate_up,
            down_weight.reshape(experts * units, depth),
            *inputs,
        )
        odd, even, far, arrived = lax.optimization_barrier((odd, even, far, arrived))
        if waiting:
            total = sum([one.astype(F32) for one in arrived], waiting[0])
            for mask, one in zip(last, total):
                if mask:
                    one = swap(one.astype(BF16), "gx", mask).astype(F32)
                result = result + one
        last = masks
        near = swap(odd, "gy", 1)
        inputs = [one for pieces in far for one in gather_near(pieces)]
        summed = even.astype(F32) + near.astype(F32)
        if after:
            waiting = [summed[0]] + [one.astype(BF16) for one in summed[1:]]
        else:
            totals, result = halve_gy([summed[:, turn] for turn in range(len(masks))], result)
    for mask, one in zip(masks, totals):
        if mask:
            one = swap(one.astype(BF16), "gx", mask).astype(F32)
        result = result + one
    return (result.astype(BF16), compacted)


def gather_far(value):
    return [value] + [swap(value, "gy", mask) for mask in range(2, lax.axis_size("gy"), 2)]


def gather_near(even):
    return [one for held in even for one in (held, swap(held, "gy", 1))]


def gather_gy(value):
    return gather_near(gather_far(value))


def far_bits(turn):
    bits = list(range(1, lax.axis_size("gy").bit_length() - 1))
    return bits[::-1] if turn else bits


def halve_gy(values, early):
    many = [[(2 * place, value[place]) for place in range(value.shape[0])] for value in values]
    orders = [far_bits(turn % 2) for turn in range(len(values))]
    for step in range(len(orders[0])):
        sent = [
            jnp.stack([one for mask, one in held if mask >> order[step] & 1]).astype(BF16)
            for held, order in zip(many, orders)
        ]
        if step + 1 == len(orders[0]):
            sent, early = lax.optimization_barrier((sent, early))
        for turn, order in enumerate(orders):
            got = swap(sent[turn], "gy", 1 << order[step]).astype(F32)
            mine = [(mask, one) for mask, one in many[turn] if not mask >> order[step] & 1]
            many[turn] = [(mask, one + got[place]) for place, (mask, one) in enumerate(mine)]
    return [held[0][1] for held in many], early


def solution(mesh):
    placed = (
        P("gx", "gy"),
        P(),
        P("gx", None, "gy"),
        P("gx", "gy"),
        P("gx", None, None, "gy"),
        P("gx"),
        P("gx"),
        P("gx", None),
        P("gx", None),
        P(),
        P("gy", None, None, "gx"),
        P("gy", "gx", None),
        P(),
        P(),
    )
    return jax.shard_map(
        per_device,
        mesh=mesh,
        in_specs=placed,
        out_specs=(P("gx", "gy"), P("gx", None, "gy")),
        check_vma=False,
    )
```

```python
import math

import jax
import jax.numpy as jnp
from jax import lax
from jax.experimental import pallas as pl
from jax.experimental.pallas import tpu as pltpu
from jax.sharding import PartitionSpec as P

HD = 128
CACHE_BLOCK = 1024
VMEM_LIMIT = 56 * 1024 * 1024
BF16 = jnp.bfloat16
F32 = jnp.float32
EXPONENT = math.log2(math.e) / math.sqrt(HD)


def vmem():
    return pl.BlockSpec(memory_space=pltpu.VMEM)


def smem():
    return pl.BlockSpec(memory_space=pltpu.SMEM)


def params():
    return pltpu.CompilerParams(vmem_limit_bytes=VMEM_LIMIT)


def swap(value, axis, mask):
    count = lax.axis_size(axis)
    return lax.ppermute(value, axis, [(one, one ^ mask) for one in range(count)])


def cost(flops, size):
    return pl.CostEstimate(flops=flops, bytes_accessed=size, transcendentals=0)


def ancestor_table(parents):
    nodes = parents.shape[-1]
    column = jnp.arange(nodes, dtype=jnp.int32)
    reach = (parents[:, :, None] == column[None, None, :]).astype(F32)
    reach = reach + jnp.eye(nodes, dtype=F32)[None]
    for _ in range((nodes - 1).bit_length()):
        reach = jnp.minimum(jnp.einsum("rij,rjk->rik", reach, reach), 1.0)
    return reach


def project_kernel(count, share, ids, gain, weight, other_weight, *refs):
    pieces, outs, scaled = refs[:count], refs[count:-1], refs[-1]
    me_x, me_y = ids[0], ids[1]
    rows, width = pieces[0].shape
    for mask, piece in enumerate(pieces):
        source = me_y ^ mask
        place, part = source // share, source % share
        block, side = place // 2, place % 2
        feature = ((me_x // 2 * 2 + side) * share + part) * width
        columns = pl.ds(pl.multiple_of(feature, width), width)
        value = (piece[...].astype(F32) * gain[:, columns]).astype(BF16)
        scaled[
            side,
            pl.ds(pl.multiple_of(block * rows, rows), rows),
            pl.ds(pl.multiple_of(part * width, width), width),
        ] = value
    blocks = len(outs) // 2
    for far in range(blocks):
        place = pl.ds(pl.multiple_of((me_x ^ (2 * far)) // 2 * rows, rows), rows)
        for which in range(3):
            value = jnp.dot(
                scaled[me_x % 2, place, :], weight[which], preferred_element_type=F32
            ) + jnp.dot(
                scaled[1 - me_x % 2, place, :], other_weight[which], preferred_element_type=F32
            )
            if which == 0:
                outs[far][...] = value.astype(outs[far].dtype)
            else:
                out = outs[blocks + far]
                out[which - 1] = value.astype(out.dtype)


def blocked_query(query, request, draft, heads):
    rows = query[request * draft : (request + 1) * draft, :]
    if heads == 1:
        return rows
    column = lax.broadcasted_iota(jnp.int32, rows.shape, 1) // HD
    return jnp.concatenate(
        [jnp.where(column == head, rows, jnp.zeros_like(rows)) for head in range(heads)], axis=0
    )


def cache_kernel(
    requests, draft, heads, parts, lengths, first, held, place, scale_of, *refs
):
    terms, (cache, top, mass, mixed, query, wide) = refs[:parts], refs[parts:]
    group, block = pl.program_id(0), pl.program_id(1)
    slots = cache.shape[2]
    size = heads * draft

    @pl.when((group == 0) & (block == 0))
    def _():
        top[...] = jnp.full(top.shape, -jnp.inf, F32)
        mass[...] = jnp.zeros(mass.shape, F32)
        mixed[...] = jnp.zeros(mixed.shape, F32)
        total = terms[0][...]
        for term in terms[1:]:
            total = total + term[...].astype(F32)
        query[...] = (total * scale_of[...]).astype(BF16)
        for request in range(requests):
            rows = pl.ds(pl.multiple_of(place[request] * size, size), size)
            wide[rows, :] = blocked_query(query[...], request, draft, heads)

    left = lengths[group] - block * slots
    for count in range(1, requests + 1):

        @pl.when((held[group] == count) & (left > 0))
        def _():
            rows = pl.ds(pl.multiple_of(first[group] * size, size), count * size)
            scores = lax.dot_general(
                wide[rows, :],
                cache[0, 0],
                (((1,), (1,)), ((), ())),
                preferred_element_type=F32,
            )
            column = lax.broadcasted_iota(jnp.int32, (1, slots), 1)
            scores = scores + jnp.where(column < left, 0.0, -jnp.inf)
            before = top[rows, :]
            now = jnp.maximum(before, jnp.max(scores, axis=1, keepdims=True))
            spread = jnp.concatenate([now] * (slots // now.shape[1]), axis=1)
            powered = jnp.exp2((scores - spread) * EXPONENT)
            fade = jnp.exp2((before - now) * EXPONENT)
            top[rows, :] = now
            mass[rows, :] = mass[rows, :] * fade + jnp.sum(powered, axis=1, keepdims=True)
            mixed[rows, :] = mixed[rows, :] * jnp.concatenate([fade] * heads, axis=1) + jnp.dot(
                powered.astype(BF16), cache[0, 1], preferred_element_type=F32
            )


def draft_kernel(requests, draft, heads, parts, count, ids, place, scale_of, *refs):
    pairs = refs[:parts]
    query, reach, rows, top, mass, mixed, output = refs[parts : parts + 7]
    even, odd, picked, key, value, attended = refs[parts + 7 :]
    me = ids[1]
    for which, kept in ((0, key), (1, value)):
        total = pairs[0][which]
        for pair in pairs[1:]:
            total = total + pair[which].astype(F32)
        kept[...] = (total * scale_of[...]).astype(BF16)
    tokens = key.shape[0]
    chosen = (
        lax.broadcasted_iota(jnp.int32, (rows.shape[0], tokens), 1) == rows[...]
    ).astype(BF16)
    picked[0] = jnp.dot(chosen, key[...], preferred_element_type=F32).astype(BF16)
    picked[1] = jnp.dot(chosen, value[...], preferred_element_type=F32).astype(BF16)
    size = heads * draft
    for request in range(requests):
        own = slice(request * draft, (request + 1) * draft)
        kept = pl.ds(pl.multiple_of(place[request] * size, size), size)
        wide = blocked_query(query[...], request, draft, heads)
        scores = lax.dot_general(
            wide, key[own, :], (((1,), (1,)), ((), ())), preferred_element_type=F32
        )
        seen = jnp.concatenate([reach[request]] * heads, axis=0)
        scores = jnp.where(seen > 0, scores, -jnp.inf)
        before = top[kept, :][:, :1]
        now = jnp.maximum(before, jnp.max(scores, axis=1, keepdims=True))
        powered = jnp.exp2((scores - now) * EXPONENT)
        fade = jnp.exp2((before - now) * EXPONENT)
        sums = mass[kept, :][:, :1] * fade + jnp.sum(powered, axis=1, keepdims=True)
        total = mixed[kept, :] * fade + jnp.dot(
            powered.astype(BF16), value[own, :], preferred_element_type=F32
        )
        total = (total / sums).astype(BF16)
        for head in range(heads):
            attended[own, head * HD : (head + 1) * HD] = total[
                head * draft : (head + 1) * draft, head * HD : (head + 1) * HD
            ]
    width = even.shape[-1]
    for mask in range(count):
        columns = pl.ds(pl.multiple_of((me ^ mask) * width, width), width)
        value = lax.dot_general(
            attended[...],
            output[columns, :],
            (((1,), (1,)), ((), ())),
            preferred_element_type=F32,
        ).astype(BF16)
        (odd if mask % 2 else even)[mask // 2] = value


def expert_kernel(count, masks, stacked, ids, gain, route, route_gate, weight, down, *refs):
    blocks = len(masks)
    pieces, (odd, even, normed, hidden, held, arrival) = refs[:-6], refs[-6:]
    me_x, me_y = ids[0], ids[1]
    rows, width = pieces[0].shape[-2:]
    step = pl.program_id(0)
    fetch = pltpu.make_async_copy(down, held, arrival)

    @pl.when(step == 0)
    def _():
        fetch.start()
        for block in range(blocks):
            if stacked:
                own = [piece.at[block] for piece in pieces]
            else:
                own = pieces[block * count : (block + 1) * count]
            place = slice(block * rows, (block + 1) * rows)
            squares = jnp.zeros((rows, 1), F32)
            for piece in own:
                value = piece[...].astype(F32)
                squares = squares + jnp.sum(value * value, axis=1, keepdims=True)
            scale = lax.rsqrt(squares / (width * count) + 1e-05)
            for mask, piece in enumerate(own):
                columns = pl.ds(pl.multiple_of((me_y ^ mask) * width, width), width)
                value = piece[...].astype(F32) * scale * gain[:, columns]
                normed[place, columns] = value.astype(BF16)

    gate = jnp.dot(normed[...], weight[0, 0], preferred_element_type=F32)
    up = jnp.dot(normed[...], weight[1, 0], preferred_element_type=F32)
    expert = me_y * pl.num_programs(0) + step
    value = gate / (1.0 + jnp.exp(-gate)) * up
    for block, mask in enumerate(masks):
        place = slice(block * rows, (block + 1) * rows)
        source = pl.ds(pl.multiple_of((me_x ^ mask) * rows, rows), rows)
        chosen = jnp.where(route[:, source] == expert, route_gate[:, source], 0.0)
        factor = lax.dot_general(
            chosen.astype(BF16),
            jnp.ones((chosen.shape[0], value.shape[1]), BF16),
            (((0,), (0,)), ((), ())),
            preferred_element_type=F32,
        )
        hidden[step, place, :] = (value[place, :] * factor).astype(BF16)

    @pl.when(step == pl.num_programs(0) - 1)
    def _():
        fetch.wait()
        every = jnp.concatenate([hidden[one] for one in range(hidden.shape[0])], axis=1)
        for mask in range(count):
            columns = pl.ds(pl.multiple_of((me_y ^ mask) * width, width), width)
            terms = jnp.dot(every, held[:, columns], preferred_element_type=F32).astype(BF16)
            for block in range(blocks):
                (odd if mask % 2 else even)[mask // 2, block] = terms[
                    block * rows : (block + 1) * rows, :
                ]


def per_device(
    tokens,
    attention_gain,
    projection_weight,
    output_weight,
    prompt_cache,
    cache_length,
    prompt_group,
    parents,
    accepted_path,
    expert_gain,
    gate_up_weight,
    down_weight,
    route_experts,
    route_gates,
):
    gx_count, gy_count = lax.axis_size("gx"), lax.axis_size("gy")
    ids = jnp.stack([lax.axis_index("gx"), lax.axis_index("gy")]).astype(jnp.int32)
    rows, width = tokens.shape
    depth = attention_gain.shape[0]
    requests, draft = parents.shape
    groups = prompt_cache.shape[0]
    heads = width // HD

    wide_tokens = tokens.astype(F32)
    squares = jnp.sum(wide_tokens * wide_tokens, axis=1, keepdims=True)
    for bit in range(gy_count.bit_length() - 1):
        squares = squares + swap(squares, "gy", 1 << bit)
    row_scale = lax.rsqrt(squares / depth + 1e-05)

    weight = jnp.transpose(projection_weight, (1, 0, 2))
    share = gy_count // gx_count
    terms_of = gx_count // 2
    route = [
        (
            a * gy_count + b,
            (b // share // 2 * 2 + a % 2) * gy_count
            + (a // 2 * 2 + b // share % 2) * share
            + b % share,
        )
        for a in range(gx_count)
        for b in range(gy_count)
    ]
    moved = lax.ppermute(tokens, ("gx", "gy"), route)
    other_weight = swap(weight, "gx", 1)
    output_weight, moved = lax.optimization_barrier((output_weight, moved))
    experts = gate_up_weight.shape[0]
    units = gate_up_weight.shape[3]
    output_full = lax.all_gather(output_weight, "gx", axis=0, tiled=True)
    far = gather_far(moved)
    gate_up, far = lax.optimization_barrier((jnp.transpose(gate_up_weight, (2, 0, 1, 3)), far))
    pieces = gather_near(far)
    types = [F32] + [BF16] * (terms_of - 1)
    projected = pl.pallas_call(
        lambda *refs: project_kernel(gy_count, share, *refs),
        out_shape=[jax.ShapeDtypeStruct((rows, width), kind) for kind in types]
        + [jax.ShapeDtypeStruct((2, rows, width), kind) for kind in types],
        in_specs=[smem()] + [vmem()] * (3 + gy_count),
        out_specs=[vmem()] * (2 * terms_of),
        scratch_shapes=[pltpu.VMEM((2, terms_of * rows, share * width), BF16)],
        compiler_params=params(),
        name="project",
    )(ids, attention_gain.reshape(1, depth), weight, other_weight, *pieces)
    query_terms, pair_terms = projected[:terms_of], projected[terms_of:]
    parents, query_terms = lax.optimization_barrier((parents, query_terms))
    query_terms = [query_terms[0]] + [
        swap(query_terms[far], "gx", 2 * far) for far in range(1, terms_of)
    ]
    pair_terms = [pair_terms[0]] + [
        swap(pair_terms[far], "gx", 2 * far) for far in range(1, terms_of)
    ]

    owner = prompt_group % groups
    order = jnp.arange(requests, dtype=jnp.int32)
    ahead = (owner[None, :] < owner[:, None]) | (
        (owner[None, :] == owner[:, None]) & (order[None, :] < order[:, None])
    )
    place = jnp.sum(ahead.astype(jnp.int32), axis=1)
    group_ids = jnp.arange(groups, dtype=jnp.int32)
    held = jnp.sum((owner[None, :] == group_ids[:, None]).astype(jnp.int32), axis=1)
    first = jnp.sum((owner[None, :] < group_ids[:, None]).astype(jnp.int32), axis=1)

    slots = prompt_cache.shape[2]
    step = min(CACHE_BLOCK, slots)
    wide_rows = heads * draft
    flat = lambda *_: (0, 0)
    top, mass, mixed, query = pl.pallas_call(
        lambda *refs: cache_kernel(requests, draft, heads, terms_of, *refs),
        grid_spec=pltpu.PrefetchScalarGridSpec(
            num_scalar_prefetch=4,
            grid=(groups, slots // step),
            in_specs=[pl.BlockSpec((rows, 1), flat)]
            + [pl.BlockSpec((rows, width), flat)] * terms_of
            + [
                pl.BlockSpec(
                    (1, 2, step, width),
                    lambda group, block, lengths, first, held, place: (
                        group,
                        0,
                        jnp.where(
                            held[group] > 0, jnp.minimum(block, (lengths[group] - 1) // step), 0
                        ),
                        0,
                    ),
                ),
            ],
            out_specs=[
                pl.BlockSpec((requests * wide_rows, HD), flat),
                pl.BlockSpec((requests * wide_rows, HD), flat),
                pl.BlockSpec((requests * wide_rows, width), flat),
                pl.BlockSpec((rows, width), flat),
            ],
            scratch_shapes=[pltpu.VMEM((requests * wide_rows, width), BF16)],
        ),
        out_shape=(
            jax.ShapeDtypeStruct((requests * wide_rows, HD), F32),
            jax.ShapeDtypeStruct((requests * wide_rows, HD), F32),
            jax.ShapeDtypeStruct((requests * wide_rows, width), F32),
            jax.ShapeDtypeStruct((rows, width), BF16),
        ),
        compiler_params=params(),
        cost_estimate=cost(20 * rows * slots * width, 4 * groups * slots * width),
        name="cache",
    )(cache_length, first, held, place, row_scale, *query_terms, prompt_cache)

    accepted = accepted_path.shape[1]
    chosen = (jnp.arange(requests, dtype=jnp.int32)[:, None] * draft + accepted_path).reshape(-1, 1)
    half = jax.ShapeDtypeStruct((gy_count // 2, rows, width), BF16)
    even, odd, picked = pl.pallas_call(
        lambda *refs: draft_kernel(requests, draft, heads, terms_of, gy_count, *refs),
        out_shape=(
            half,
            half,
            jax.ShapeDtypeStruct((2, requests * accepted, width), BF16),
        ),
        in_specs=[smem(), smem()] + [vmem()] * (terms_of + 8),
        out_specs=(vmem(), vmem(), vmem()),
        scratch_shapes=[pltpu.VMEM((rows, width), BF16)] * 3,
        compiler_params=params(),
        name="draft",
    )(
        ids,
        place,
        row_scale,
        *pair_terms,
        query,
        ancestor_table(parents),
        chosen,
        top,
        mass,
        mixed,
        output_full,
    )
    compacted = jnp.transpose(picked, (1, 0, 2))

    summed = even.astype(F32) + swap(odd, "gy", 1).astype(F32)
    stream = tokens.astype(F32) + summed[0]
    for place in range(1, gy_count // 2):
        stream = stream + swap(summed[place].astype(BF16), "gy", 2 * place).astype(F32)
    stream = stream.astype(BF16)

    units_of = [(one, one + 2) for one in range(gx_count) if not one & 2]
    blocks = {0: stream, units_of[0][1]: swap(stream, "gx", units_of[0][1])}
    later, blocks[units_of[0][1]] = lax.optimization_barrier((stream, blocks[units_of[0][1]]))
    for mask in range(gx_count):
        if mask not in blocks:
            blocks[mask] = swap(later, "gx", mask)
    inputs = [one for mask in units_of[0] for one in gather_gy(blocks[mask])]
    result = stream.astype(F32)
    waiting, last = [], None
    half = jax.ShapeDtypeStruct((gy_count // 2, 2, rows, width), BF16)
    for number, masks in enumerate(units_of):
        after = []
        if number + 1 < len(units_of):
            after = [jnp.stack([blocks[mask] for mask in units_of[number + 1]])]
        inputs, waiting, after = lax.optimization_barrier((inputs, waiting, after))
        far = [gather_far(one) for one in after]
        arrived = [swap(one, "gy", 2 * place) for place, one in enumerate(waiting) if place]
        odd, even = pl.pallas_call(
            lambda *refs: expert_kernel(gy_count, masks, number > 0, *refs),
            grid=(experts,),
            in_specs=[
                smem(),
                pl.BlockSpec((1, depth), lambda expert: (0, 0)),
                vmem(),
                vmem(),
                pl.BlockSpec((2, 1, depth, units), lambda expert: (0, expert, 0, 0)),
                pl.BlockSpec(memory_space=pl.ANY),
            ]
            + [vmem()] * len(inputs),
            out_specs=[vmem(), vmem()],
            out_shape=(half, half),
            scratch_shapes=[
                pltpu.VMEM((2 * rows, depth), BF16),
                pltpu.VMEM((experts, 2 * rows, units), BF16),
                pltpu.VMEM((experts * units, depth), BF16),
                pltpu.SemaphoreType.DMA,
            ],
            compiler_params=params(),
            cost_estimate=cost(12 * rows * depth * experts * units, 6 * depth * experts * units),
            name="experts",
        )(
            ids,
            expert_gain.reshape(1, depth),
            route_experts.T,
            route_gates.astype(F32).T,
            gate_up,
            down_weight.reshape(experts * units, depth),
            *inputs,
        )
        odd, even, far, arrived = lax.optimization_barrier((odd, even, far, arrived))
        if waiting:
            total = sum([one.astype(F32) for one in arrived], waiting[0])
            for mask, one in zip(last, total):
                if mask:
                    one = swap(one.astype(BF16), "gx", mask).astype(F32)
                result = result + one
        last = masks
        near = swap(odd, "gy", 1)
        inputs = [one for pieces in far for one in gather_near(pieces)]
        summed = even.astype(F32) + near.astype(F32)
        if after:
            waiting = [summed[0]] + [one.astype(BF16) for one in summed[1:]]
        else:
            totals, result = halve_gy([summed[:, turn] for turn in range(len(masks))], result)
    for mask, one in zip(masks, totals):
        if mask:
            one = swap(one.astype(BF16), "gx", mask).astype(F32)
        result = result + one
    return (result.astype(BF16), compacted)


def gather_far(value):
    return [value] + [swap(value, "gy", mask) for mask in range(2, lax.axis_size("gy"), 2)]


def gather_near(even):
    return [one for held in even for one in (held, swap(held, "gy", 1))]


def gather_gy(value):
    return gather_near(gather_far(value))


def far_bits(turn):
    bits = list(range(1, lax.axis_size("gy").bit_length() - 1))
    return bits[::-1] if turn else bits


def halve_gy(values, early):
    many = [[(2 * place, value[place]) for place in range(value.shape[0])] for value in values]
    orders = [far_bits(turn % 2) for turn in range(len(values))]
    for step in range(len(orders[0])):
        sent = [
            jnp.stack([one for mask, one in held if mask >> order[step] & 1]).astype(BF16)
            for held, order in zip(many, orders)
        ]
        if step + 1 == len(orders[0]):
            sent, early = lax.optimization_barrier((sent, early))
        for turn, order in enumerate(orders):
            got = swap(sent[turn], "gy", 1 << order[step]).astype(F32)
            mine = [(mask, one) for mask, one in many[turn] if not mask >> order[step] & 1]
            many[turn] = [(mask, one + got[place]) for place, (mask, one) in enumerate(mine)]
    return [held[0][1] for held in many], early


def solution(mesh):
    placed = (
        P("gx", "gy"),
        P(),
        P("gx", None, "gy"),
        P("gx", "gy"),
        P("gx", None, None, "gy"),
        P("gx"),
        P("gx"),
        P("gx", None),
        P("gx", None),
        P(),
        P("gy", None, None, "gx"),
        P("gy", "gx", None),
        P(),
        P(),
    )
    return jax.shard_map(
        per_device,
        mesh=mesh,
        in_specs=placed,
        out_specs=(P("gx", "gy"), P("gx", None, "gy")),
        check_vma=False,
    )
```

```python
import math

import jax
import jax.numpy as jnp
from jax import lax
from jax.experimental import pallas as pl
from jax.experimental.pallas import tpu as pltpu
from jax.sharding import PartitionSpec as P

HD = 128
CACHE_BLOCK = 1024
VMEM_LIMIT = 56 * 1024 * 1024
BF16 = jnp.bfloat16
F32 = jnp.float32
EXPONENT = math.log2(math.e) / math.sqrt(HD)


def vmem():
    return pl.BlockSpec(memory_space=pltpu.VMEM)


def smem():
    return pl.BlockSpec(memory_space=pltpu.SMEM)


def params():
    return pltpu.CompilerParams(vmem_limit_bytes=VMEM_LIMIT)


def swap(value, axis, mask):
    count = lax.axis_size(axis)
    return lax.ppermute(value, axis, [(one, one ^ mask) for one in range(count)])


def cost(flops, size):
    return pl.CostEstimate(flops=flops, bytes_accessed=size, transcendentals=0)


def ancestor_table(parents):
    nodes = parents.shape[-1]
    column = jnp.arange(nodes, dtype=jnp.int32)
    reach = (parents[:, :, None] == column[None, None, :]).astype(F32)
    reach = reach + jnp.eye(nodes, dtype=F32)[None]
    for _ in range((nodes - 1).bit_length()):
        reach = jnp.minimum(jnp.einsum("rij,rjk->rik", reach, reach), 1.0)
    return reach


def project_kernel(count, share, ids, gain, weight, other_weight, *refs):
    pieces, outs, scaled = refs[:count], refs[count:-1], refs[-1]
    me_x, me_y = ids[0], ids[1]
    rows, width = pieces[0].shape
    for mask, piece in enumerate(pieces):
        source = me_y ^ mask
        place, part = source // share, source % share
        block, side = place // 2, place % 2
        feature = ((me_x // 2 * 2 + side) * share + part) * width
        columns = pl.ds(pl.multiple_of(feature, width), width)
        value = (piece[...].astype(F32) * gain[:, columns]).astype(BF16)
        scaled[
            side,
            pl.ds(pl.multiple_of(block * rows, rows), rows),
            pl.ds(pl.multiple_of(part * width, width), width),
        ] = value
    blocks = len(outs) // 2
    for far in range(blocks):
        place = pl.ds(pl.multiple_of((me_x ^ (2 * far)) // 2 * rows, rows), rows)
        for which in range(3):
            value = jnp.dot(
                scaled[me_x % 2, place, :], weight[which], preferred_element_type=F32
            ) + jnp.dot(
                scaled[1 - me_x % 2, place, :], other_weight[which], preferred_element_type=F32
            )
            if which == 0:
                outs[far][...] = value.astype(outs[far].dtype)
            else:
                out = outs[blocks + far]
                out[which - 1] = value.astype(out.dtype)


def blocked_query(query, request, draft, heads):
    rows = query[request * draft : (request + 1) * draft, :]
    if heads == 1:
        return rows
    column = lax.broadcasted_iota(jnp.int32, rows.shape, 1) // HD
    return jnp.concatenate(
        [jnp.where(column == head, rows, jnp.zeros_like(rows)) for head in range(heads)], axis=0
    )


def cache_kernel(
    requests, draft, heads, parts, lengths, first, held, place, scale_of, *refs
):
    terms, (cache, top, mass, mixed, query, wide) = refs[:parts], refs[parts:]
    group, block = pl.program_id(0), pl.program_id(1)
    slots = cache.shape[2]
    size = heads * draft

    @pl.when((group == 0) & (block == 0))
    def _():
        top[...] = jnp.full(top.shape, -jnp.inf, F32)
        mass[...] = jnp.zeros(mass.shape, F32)
        mixed[...] = jnp.zeros(mixed.shape, F32)
        total = terms[0][...]
        for term in terms[1:]:
            total = total + term[...].astype(F32)
        query[...] = (total * scale_of[...]).astype(BF16)
        for request in range(requests):
            rows = pl.ds(pl.multiple_of(place[request] * size, size), size)
            wide[rows, :] = blocked_query(query[...], request, draft, heads)

    left = lengths[group] - block * slots
    for count in range(1, requests + 1):

        @pl.when((held[group] == count) & (left > 0))
        def _():
            rows = pl.ds(pl.multiple_of(first[group] * size, size), count * size)
            scores = lax.dot_general(
                wide[rows, :],
                cache[0, 0],
                (((1,), (1,)), ((), ())),
                preferred_element_type=F32,
            )
            column = lax.broadcasted_iota(jnp.int32, (1, slots), 1)
            scores = scores + jnp.where(column < left, 0.0, -jnp.inf)
            before = top[rows, :]
            now = jnp.maximum(before, jnp.max(scores, axis=1, keepdims=True))
            spread = jnp.concatenate([now] * (slots // now.shape[1]), axis=1)
            powered = jnp.exp2((scores - spread) * EXPONENT)
            fade = jnp.exp2((before - now) * EXPONENT)
            top[rows, :] = now
            mass[rows, :] = mass[rows, :] * fade + jnp.sum(powered, axis=1, keepdims=True)
            mixed[rows, :] = mixed[rows, :] * jnp.concatenate([fade] * heads, axis=1) + jnp.dot(
                powered.astype(BF16), cache[0, 1], preferred_element_type=F32
            )


def draft_kernel(requests, draft, heads, parts, count, ids, place, scale_of, *refs):
    pairs = refs[:parts]
    query, reach, rows, top, mass, mixed, output = refs[parts : parts + 7]
    even, odd, picked, key, value, attended = refs[parts + 7 :]
    me = ids[1]
    for which, kept in ((0, key), (1, value)):
        total = pairs[0][which]
        for pair in pairs[1:]:
            total = total + pair[which].astype(F32)
        kept[...] = (total * scale_of[...]).astype(BF16)
    tokens = key.shape[0]
    chosen = (
        lax.broadcasted_iota(jnp.int32, (rows.shape[0], tokens), 1) == rows[...]
    ).astype(BF16)
    picked[0] = jnp.dot(chosen, key[...], preferred_element_type=F32).astype(BF16)
    picked[1] = jnp.dot(chosen, value[...], preferred_element_type=F32).astype(BF16)
    size = heads * draft
    for request in range(requests):
        own = slice(request * draft, (request + 1) * draft)
        kept = pl.ds(pl.multiple_of(place[request] * size, size), size)
        wide = blocked_query(query[...], request, draft, heads)
        scores = lax.dot_general(
            wide, key[own, :], (((1,), (1,)), ((), ())), preferred_element_type=F32
        )
        seen = jnp.concatenate([reach[request]] * heads, axis=0)
        scores = jnp.where(seen > 0, scores, -jnp.inf)
        before = top[kept, :][:, :1]
        now = jnp.maximum(before, jnp.max(scores, axis=1, keepdims=True))
        powered = jnp.exp2((scores - now) * EXPONENT)
        fade = jnp.exp2((before - now) * EXPONENT)
        sums = mass[kept, :][:, :1] * fade + jnp.sum(powered, axis=1, keepdims=True)
        total = mixed[kept, :] * fade + jnp.dot(
            powered.astype(BF16), value[own, :], preferred_element_type=F32
        )
        total = (total / sums).astype(BF16)
        for head in range(heads):
            attended[own, head * HD : (head + 1) * HD] = total[
                head * draft : (head + 1) * draft, head * HD : (head + 1) * HD
            ]
    width = even.shape[-1]
    for mask in range(count):
        columns = pl.ds(pl.multiple_of((me ^ mask) * width, width), width)
        value = lax.dot_general(
            attended[...],
            output[columns, :],
            (((1,), (1,)), ((), ())),
            preferred_element_type=F32,
        ).astype(BF16)
        (odd if mask % 2 else even)[mask // 2] = value


def expert_kernel(count, masks, stacked, ids, gain, route, route_gate, weight, down, *refs):
    blocks = len(masks)
    pieces, (odd, even, normed, hidden, held, arrival) = refs[:-6], refs[-6:]
    me_x, me_y = ids[0], ids[1]
    rows, width = pieces[0].shape[-2:]
    step = pl.program_id(0)
    fetch = pltpu.make_async_copy(down, held, arrival)

    @pl.when(step == 0)
    def _():
        fetch.start()
        for block in range(blocks):
            if stacked:
                own = [piece.at[block] for piece in pieces]
            else:
                own = pieces[block * count : (block + 1) * count]
            place = slice(block * rows, (block + 1) * rows)
            squares = jnp.zeros((rows, 1), F32)
            for piece in own:
                value = piece[...].astype(F32)
                squares = squares + jnp.sum(value * value, axis=1, keepdims=True)
            scale = lax.rsqrt(squares / (width * count) + 1e-05)
            for mask, piece in enumerate(own):
                columns = pl.ds(pl.multiple_of((me_y ^ mask) * width, width), width)
                value = piece[...].astype(F32) * scale * gain[:, columns]
                normed[place, columns] = value.astype(BF16)

    gate = jnp.dot(normed[...], weight[0, 0], preferred_element_type=F32)
    up = jnp.dot(normed[...], weight[1, 0], preferred_element_type=F32)
    expert = me_y * pl.num_programs(0) + step
    value = gate / (1.0 + jnp.exp(-gate)) * up
    for block, mask in enumerate(masks):
        place = slice(block * rows, (block + 1) * rows)
        source = pl.ds(pl.multiple_of((me_x ^ mask) * rows, rows), rows)
        chosen = jnp.where(route[:, source] == expert, route_gate[:, source], 0.0)
        factor = lax.dot_general(
            chosen.astype(BF16),
            jnp.ones((chosen.shape[0], value.shape[1]), BF16),
            (((0,), (0,)), ((), ())),
            preferred_element_type=F32,
        )
        hidden[step, place, :] = (value[place, :] * factor).astype(BF16)

    @pl.when(step == pl.num_programs(0) - 1)
    def _():
        fetch.wait()
        every = jnp.concatenate([hidden[one] for one in range(hidden.shape[0])], axis=1)
        for mask in range(count):
            columns = pl.ds(pl.multiple_of((me_y ^ mask) * width, width), width)
            terms = jnp.dot(every, held[:, columns], preferred_element_type=F32).astype(BF16)
            for block in range(blocks):
                (odd if mask % 2 else even)[mask // 2, block] = terms[
                    block * rows : (block + 1) * rows, :
                ]


def per_device(
    tokens,
    attention_gain,
    projection_weight,
    output_weight,
    prompt_cache,
    cache_length,
    prompt_group,
    parents,
    accepted_path,
    expert_gain,
    gate_up_weight,
    down_weight,
    route_experts,
    route_gates,
):
    gx_count, gy_count = lax.axis_size("gx"), lax.axis_size("gy")
    ids = jnp.stack([lax.axis_index("gx"), lax.axis_index("gy")]).astype(jnp.int32)
    rows, width = tokens.shape
    depth = attention_gain.shape[0]
    requests, draft = parents.shape
    groups = prompt_cache.shape[0]
    heads = width // HD

    wide_tokens = tokens.astype(F32)
    squares = jnp.sum(wide_tokens * wide_tokens, axis=1, keepdims=True)
    for bit in range(gy_count.bit_length() - 1):
        squares = squares + swap(squares, "gy", 1 << bit)
    row_scale = lax.rsqrt(squares / depth + 1e-05)

    weight = jnp.transpose(projection_weight, (1, 0, 2))
    share = gy_count // gx_count
    terms_of = gx_count // 2
    route = [
        (
            a * gy_count + b,
            (b // share // 2 * 2 + a % 2) * gy_count
            + (a // 2 * 2 + b // share % 2) * share
            + b % share,
        )
        for a in range(gx_count)
        for b in range(gy_count)
    ]
    moved = lax.ppermute(tokens, ("gx", "gy"), route)
    other_weight = swap(weight, "gx", 1)
    experts = gate_up_weight.shape[0]
    units = gate_up_weight.shape[3]
    output_full = lax.all_gather(output_weight, "gx", axis=0, tiled=True)
    far = gather_far(moved)
    gate_up, far = lax.optimization_barrier((jnp.transpose(gate_up_weight, (2, 0, 1, 3)), far))
    pieces = gather_near(far)
    types = [F32] + [BF16] * (terms_of - 1)
    projected = pl.pallas_call(
        lambda *refs: project_kernel(gy_count, share, *refs),
        out_shape=[jax.ShapeDtypeStruct((rows, width), kind) for kind in types]
        + [jax.ShapeDtypeStruct((2, rows, width), kind) for kind in types],
        in_specs=[smem()] + [vmem()] * (3 + gy_count),
        out_specs=[vmem()] * (2 * terms_of),
        scratch_shapes=[pltpu.VMEM((2, terms_of * rows, share * width), BF16)],
        compiler_params=params(),
        name="project",
    )(ids, attention_gain.reshape(1, depth), weight, other_weight, *pieces)
    query_terms, pair_terms = projected[:terms_of], projected[terms_of:]
    parents, query_terms = lax.optimization_barrier((parents, query_terms))
    query_terms = [query_terms[0]] + [
        swap(query_terms[far], "gx", 2 * far) for far in range(1, terms_of)
    ]
    pair_terms = [pair_terms[0]] + [
        swap(pair_terms[far], "gx", 2 * far) for far in range(1, terms_of)
    ]

    owner = prompt_group % groups
    order = jnp.arange(requests, dtype=jnp.int32)
    ahead = (owner[None, :] < owner[:, None]) | (
        (owner[None, :] == owner[:, None]) & (order[None, :] < order[:, None])
    )
    place = jnp.sum(ahead.astype(jnp.int32), axis=1)
    group_ids = jnp.arange(groups, dtype=jnp.int32)
    held = jnp.sum((owner[None, :] == group_ids[:, None]).astype(jnp.int32), axis=1)
    first = jnp.sum((owner[None, :] < group_ids[:, None]).astype(jnp.int32), axis=1)

    slots = prompt_cache.shape[2]
    step = min(CACHE_BLOCK, slots)
    wide_rows = heads * draft
    flat = lambda *_: (0, 0)
    top, mass, mixed, query = pl.pallas_call(
        lambda *refs: cache_kernel(requests, draft, heads, terms_of, *refs),
        grid_spec=pltpu.PrefetchScalarGridSpec(
            num_scalar_prefetch=4,
            grid=(groups, slots // step),
            in_specs=[pl.BlockSpec((rows, 1), flat)]
            + [pl.BlockSpec((rows, width), flat)] * terms_of
            + [
                pl.BlockSpec(
                    (1, 2, step, width),
                    lambda group, block, lengths, first, held, place: (
                        group,
                        0,
                        jnp.where(
                            held[group] > 0, jnp.minimum(block, (lengths[group] - 1) // step), 0
                        ),
                        0,
                    ),
                ),
            ],
            out_specs=[
                pl.BlockSpec((requests * wide_rows, HD), flat),
                pl.BlockSpec((requests * wide_rows, HD), flat),
                pl.BlockSpec((requests * wide_rows, width), flat),
                pl.BlockSpec((rows, width), flat),
            ],
            scratch_shapes=[pltpu.VMEM((requests * wide_rows, width), BF16)],
        ),
        out_shape=(
            jax.ShapeDtypeStruct((requests * wide_rows, HD), F32),
            jax.ShapeDtypeStruct((requests * wide_rows, HD), F32),
            jax.ShapeDtypeStruct((requests * wide_rows, width), F32),
            jax.ShapeDtypeStruct((rows, width), BF16),
        ),
        compiler_params=params(),
        cost_estimate=cost(20 * rows * slots * width, 4 * groups * slots * width),
        name="cache",
    )(cache_length, first, held, place, row_scale, *query_terms, prompt_cache)

    accepted = accepted_path.shape[1]
    chosen = (jnp.arange(requests, dtype=jnp.int32)[:, None] * draft + accepted_path).reshape(-1, 1)
    half = jax.ShapeDtypeStruct((gy_count // 2, rows, width), BF16)
    even, odd, picked = pl.pallas_call(
        lambda *refs: draft_kernel(requests, draft, heads, terms_of, gy_count, *refs),
        out_shape=(
            half,
            half,
            jax.ShapeDtypeStruct((2, requests * accepted, width), BF16),
        ),
        in_specs=[smem(), smem()] + [vmem()] * (terms_of + 8),
        out_specs=(vmem(), vmem(), vmem()),
        scratch_shapes=[pltpu.VMEM((rows, width), BF16)] * 3,
        compiler_params=params(),
        name="draft",
    )(
        ids,
        place,
        row_scale,
        *pair_terms,
        query,
        ancestor_table(parents),
        chosen,
        top,
        mass,
        mixed,
        output_full,
    )
    compacted = jnp.transpose(picked, (1, 0, 2))

    summed = even.astype(F32) + swap(odd, "gy", 1).astype(F32)
    stream = tokens.astype(F32) + summed[0]
    for place in range(1, gy_count // 2):
        stream = stream + swap(summed[place].astype(BF16), "gy", 2 * place).astype(F32)
    stream = stream.astype(BF16)

    units_of = [(one, one + 2) for one in range(gx_count) if not one & 2]
    blocks = {0: stream, units_of[0][1]: swap(stream, "gx", units_of[0][1])}
    later, blocks[units_of[0][1]] = lax.optimization_barrier((stream, blocks[units_of[0][1]]))
    for mask in range(gx_count):
        if mask not in blocks:
            blocks[mask] = swap(later, "gx", mask)
    inputs = [one for mask in units_of[0] for one in gather_gy(blocks[mask])]
    result = stream.astype(F32)
    waiting, last = [], None
    half = jax.ShapeDtypeStruct((gy_count // 2, 2, rows, width), BF16)
    for number, masks in enumerate(units_of):
        after = []
        if number + 1 < len(units_of):
            after = [jnp.stack([blocks[mask] for mask in units_of[number + 1]])]
        inputs, waiting, after = lax.optimization_barrier((inputs, waiting, after))
        far = [gather_far(one) for one in after]
        arrived = [swap(one, "gy", 2 * place) for place, one in enumerate(waiting) if place]
        odd, even = pl.pallas_call(
            lambda *refs: expert_kernel(gy_count, masks, number > 0, *refs),
            grid=(experts,),
            in_specs=[
                smem(),
                pl.BlockSpec((1, depth), lambda expert: (0, 0)),
                vmem(),
                vmem(),
                pl.BlockSpec((2, 1, depth, units), lambda expert: (0, expert, 0, 0)),
                pl.BlockSpec(memory_space=pl.ANY),
            ]
            + [vmem()] * len(inputs),
            out_specs=[vmem(), vmem()],
            out_shape=(half, half),
            scratch_shapes=[
                pltpu.VMEM((2 * rows, depth), BF16),
                pltpu.VMEM((experts, 2 * rows, units), BF16),
                pltpu.VMEM((experts * units, depth), BF16),
                pltpu.SemaphoreType.DMA,
            ],
            compiler_params=params(),
            cost_estimate=cost(12 * rows * depth * experts * units, 6 * depth * experts * units),
            name="experts",
        )(
            ids,
            expert_gain.reshape(1, depth),
            route_experts.T,
            route_gates.astype(F32).T,
            gate_up,
            down_weight.reshape(experts * units, depth),
            *inputs,
        )
        odd, even, far, arrived = lax.optimization_barrier((odd, even, far, arrived))
        if waiting:
            total = sum([one.astype(F32) for one in arrived], waiting[0])
            for mask, one in zip(last, total):
                if mask:
                    one = swap(one.astype(BF16), "gx", mask).astype(F32)
                result = result + one
        last = masks
        near = swap(odd, "gy", 1)
        inputs = [one for pieces in far for one in gather_near(pieces)]
        summed = even.astype(F32) + near.astype(F32)
        if after:
            waiting = [summed[0]] + [one.astype(BF16) for one in summed[1:]]
        else:
            totals, result = halve_gy([summed[:, turn] for turn in range(len(masks))], result)
    for mask, one in zip(masks, totals):
        if mask:
            one = swap(one.astype(BF16), "gx", mask).astype(F32)
        result = result + one
    return (result.astype(BF16), compacted)


def gather_far(value):
    return [value] + [swap(value, "gy", mask) for mask in range(2, lax.axis_size("gy"), 2)]


def gather_near(even):
    return [one for held in even for one in (held, swap(held, "gy", 1))]


def gather_gy(value):
    return gather_near(gather_far(value))


def far_bits(turn):
    bits = list(range(1, lax.axis_size("gy").bit_length() - 1))
    return bits[::-1] if turn else bits


def halve_gy(values, early):
    many = [[(2 * place, value[place]) for place in range(value.shape[0])] for value in values]
    orders = [far_bits(turn % 2) for turn in range(len(values))]
    for step in range(len(orders[0])):
        sent = [
            jnp.stack([one for mask, one in held if mask >> order[step] & 1]).astype(BF16)
            for held, order in zip(many, orders)
        ]
        if step + 1 == len(orders[0]):
            sent, early = lax.optimization_barrier((sent, early))
        for turn, order in enumerate(orders):
            got = swap(sent[turn], "gy", 1 << order[step]).astype(F32)
            mine = [(mask, one) for mask, one in many[turn] if not mask >> order[step] & 1]
            many[turn] = [(mask, one + got[place]) for place, (mask, one) in enumerate(mine)]
    return [held[0][1] for held in many], early


def solution(mesh):
    placed = (
        P("gx", "gy"),
        P(),
        P("gx", None, "gy"),
        P("gx", "gy"),
        P("gx", None, None, "gy"),
        P("gx"),
        P("gx"),
        P("gx", None),
        P("gx", None),
        P(),
        P("gy", None, None, "gx"),
        P("gy", "gx", None),
        P(),
        P(),
    )
    return jax.shard_map(
        per_device,
        mesh=mesh,
        in_specs=placed,
        out_specs=(P("gx", "gy"), P("gx", None, "gy")),
        check_vma=False,
    )
```

```python
import math

import jax
import jax.numpy as jnp
from jax import lax
from jax.experimental import pallas as pl
from jax.experimental.pallas import tpu as pltpu
from jax.sharding import PartitionSpec as P

HD = 128
CACHE_BLOCK = 1024
VMEM_LIMIT = 56 * 1024 * 1024
BF16 = jnp.bfloat16
F32 = jnp.float32
EXPONENT = math.log2(math.e) / math.sqrt(HD)


def vmem():
    return pl.BlockSpec(memory_space=pltpu.VMEM)


def smem():
    return pl.BlockSpec(memory_space=pltpu.SMEM)


def params():
    return pltpu.CompilerParams(vmem_limit_bytes=VMEM_LIMIT)


def swap(value, axis, mask):
    count = lax.axis_size(axis)
    return lax.ppermute(value, axis, [(one, one ^ mask) for one in range(count)])


def cost(flops, size):
    return pl.CostEstimate(flops=flops, bytes_accessed=size, transcendentals=0)


def ancestor_table(parents):
    nodes = parents.shape[-1]
    column = jnp.arange(nodes, dtype=jnp.int32)
    reach = (parents[:, :, None] == column[None, None, :]).astype(F32)
    reach = reach + jnp.eye(nodes, dtype=F32)[None]
    for _ in range((nodes - 1).bit_length()):
        reach = jnp.minimum(jnp.einsum("rij,rjk->rik", reach, reach), 1.0)
    return reach


def project_kernel(count, share, ids, gain, weight, other_weight, *refs):
    pieces, outs, scaled = refs[:count], refs[count:-1], refs[-1]
    me_x, me_y = ids[0], ids[1]
    rows, width = pieces[0].shape
    for mask, piece in enumerate(pieces):
        source = me_y ^ mask
        place, part = source // share, source % share
        block, side = place // 2, place % 2
        feature = ((me_x // 2 * 2 + side) * share + part) * width
        columns = pl.ds(pl.multiple_of(feature, width), width)
        value = (piece[...].astype(F32) * gain[:, columns]).astype(BF16)
        scaled[
            side,
            pl.ds(pl.multiple_of(block * rows, rows), rows),
            pl.ds(pl.multiple_of(part * width, width), width),
        ] = value
    blocks = len(outs) // 2
    for far in range(blocks):
        place = pl.ds(pl.multiple_of((me_x ^ (2 * far)) // 2 * rows, rows), rows)
        for which in range(3):
            value = jnp.dot(
                scaled[me_x % 2, place, :], weight[which], preferred_element_type=F32
            ) + jnp.dot(
                scaled[1 - me_x % 2, place, :], other_weight[which], preferred_element_type=F32
            )
            if which == 0:
                outs[far][...] = value.astype(outs[far].dtype)
            else:
                out = outs[blocks + far]
                out[which - 1] = value.astype(out.dtype)


def blocked_query(query, request, draft, heads):
    rows = query[request * draft : (request + 1) * draft, :]
    if heads == 1:
        return rows
    column = lax.broadcasted_iota(jnp.int32, rows.shape, 1) // HD
    return jnp.concatenate(
        [jnp.where(column == head, rows, jnp.zeros_like(rows)) for head in range(heads)], axis=0
    )


def cache_kernel(
    requests, draft, heads, parts, lengths, first, held, place, scale_of, *refs
):
    terms, (cache, top, mass, mixed, query, wide) = refs[:parts], refs[parts:]
    group, block = pl.program_id(0), pl.program_id(1)
    slots = cache.shape[2]
    size = heads * draft

    @pl.when((group == 0) & (block == 0))
    def _():
        top[...] = jnp.full(top.shape, -jnp.inf, F32)
        mass[...] = jnp.zeros(mass.shape, F32)
        mixed[...] = jnp.zeros(mixed.shape, F32)
        total = terms[0][...]
        for term in terms[1:]:
            total = total + term[...].astype(F32)
        query[...] = (total * scale_of[...]).astype(BF16)
        for request in range(requests):
            rows = pl.ds(pl.multiple_of(place[request] * size, size), size)
            wide[rows, :] = blocked_query(query[...], request, draft, heads)

    left = lengths[group] - block * slots
    for count in range(1, requests + 1):

        @pl.when((held[group] == count) & (left > 0))
        def _():
            rows = pl.ds(pl.multiple_of(first[group] * size, size), count * size)
            scores = lax.dot_general(
                wide[rows, :],
                cache[0, 0],
                (((1,), (1,)), ((), ())),
                preferred_element_type=F32,
            )
            column = lax.broadcasted_iota(jnp.int32, (1, slots), 1)
            scores = scores + jnp.where(column < left, 0.0, -jnp.inf)
            before = top[rows, :]
            now = jnp.maximum(before, jnp.max(scores, axis=1, keepdims=True))
            spread = jnp.concatenate([now] * (slots // now.shape[1]), axis=1)
            powered = jnp.exp2((scores - spread) * EXPONENT)
            fade = jnp.exp2((before - now) * EXPONENT)
            top[rows, :] = now
            mass[rows, :] = mass[rows, :] * fade + jnp.sum(powered, axis=1, keepdims=True)
            mixed[rows, :] = mixed[rows, :] * jnp.concatenate([fade] * heads, axis=1) + jnp.dot(
                powered.astype(BF16), cache[0, 1], preferred_element_type=F32
            )


def draft_kernel(requests, draft, heads, parts, count, ids, place, scale_of, *refs):
    pairs = refs[:parts]
    query, reach, rows, top, mass, mixed = refs[parts : parts + 6]
    blocks = refs[parts + 6 : -7]
    even, odd, picked, key, value, attended, output = refs[-7:]
    me = ids[1]
    depth = blocks[0].shape[0]
    for mask, one in enumerate(blocks):
        output[pl.ds(pl.multiple_of((ids[0] ^ mask) * depth, depth), depth), :] = one[...]
    for which, kept in ((0, key), (1, value)):
        total = pairs[0][which]
        for pair in pairs[1:]:
            total = total + pair[which].astype(F32)
        kept[...] = (total * scale_of[...]).astype(BF16)
    tokens = key.shape[0]
    chosen = (
        lax.broadcasted_iota(jnp.int32, (rows.shape[0], tokens), 1) == rows[...]
    ).astype(BF16)
    picked[0] = jnp.dot(chosen, key[...], preferred_element_type=F32).astype(BF16)
    picked[1] = jnp.dot(chosen, value[...], preferred_element_type=F32).astype(BF16)
    size = heads * draft
    for request in range(requests):
        own = slice(request * draft, (request + 1) * draft)
        kept = pl.ds(pl.multiple_of(place[request] * size, size), size)
        wide = blocked_query(query[...], request, draft, heads)
        scores = lax.dot_general(
            wide, key[own, :], (((1,), (1,)), ((), ())), preferred_element_type=F32
        )
        seen = jnp.concatenate([reach[request]] * heads, axis=0)
        scores = jnp.where(seen > 0, scores, -jnp.inf)
        before = top[kept, :][:, :1]
        now = jnp.maximum(before, jnp.max(scores, axis=1, keepdims=True))
        powered = jnp.exp2((scores - now) * EXPONENT)
        fade = jnp.exp2((before - now) * EXPONENT)
        sums = mass[kept, :][:, :1] * fade + jnp.sum(powered, axis=1, keepdims=True)
        total = mixed[kept, :] * fade + jnp.dot(
            powered.astype(BF16), value[own, :], preferred_element_type=F32
        )
        total = (total / sums).astype(BF16)
        for head in range(heads):
            attended[own, head * HD : (head + 1) * HD] = total[
                head * draft : (head + 1) * draft, head * HD : (head + 1) * HD
            ]
    width = even.shape[-1]
    for mask in range(count):
        columns = pl.ds(pl.multiple_of((me ^ mask) * width, width), width)
        value = lax.dot_general(
            attended[...],
            output[columns, :],
            (((1,), (1,)), ((), ())),
            preferred_element_type=F32,
        ).astype(BF16)
        (odd if mask % 2 else even)[mask // 2] = value


def expert_kernel(count, masks, stacked, ids, gain, route, route_gate, weight, down, *refs):
    blocks = len(masks)
    pieces, (odd, even, normed, hidden, held, arrival) = refs[:-6], refs[-6:]
    me_x, me_y = ids[0], ids[1]
    rows, width = pieces[0].shape[-2:]
    step = pl.program_id(0)
    fetch = pltpu.make_async_copy(down, held, arrival)

    @pl.when(step == 0)
    def _():
        fetch.start()
        for block in range(blocks):
            if stacked:
                own = [piece.at[block] for piece in pieces]
            else:
                own = pieces[block * count : (block + 1) * count]
            place = slice(block * rows, (block + 1) * rows)
            squares = jnp.zeros((rows, 1), F32)
            for piece in own:
                value = piece[...].astype(F32)
                squares = squares + jnp.sum(value * value, axis=1, keepdims=True)
            scale = lax.rsqrt(squares / (width * count) + 1e-05)
            for mask, piece in enumerate(own):
                columns = pl.ds(pl.multiple_of((me_y ^ mask) * width, width), width)
                value = piece[...].astype(F32) * scale * gain[:, columns]
                normed[place, columns] = value.astype(BF16)

    gate = jnp.dot(normed[...], weight[0, 0], preferred_element_type=F32)
    up = jnp.dot(normed[...], weight[1, 0], preferred_element_type=F32)
    expert = me_y * pl.num_programs(0) + step
    value = gate / (1.0 + jnp.exp(-gate)) * up
    for block, mask in enumerate(masks):
        place = slice(block * rows, (block + 1) * rows)
        source = pl.ds(pl.multiple_of((me_x ^ mask) * rows, rows), rows)
        chosen = jnp.where(route[:, source] == expert, route_gate[:, source], 0.0)
        factor = lax.dot_general(
            chosen.astype(BF16),
            jnp.ones((chosen.shape[0], value.shape[1]), BF16),
            (((0,), (0,)), ((), ())),
            preferred_element_type=F32,
        )
        hidden[step, place, :] = (value[place, :] * factor).astype(BF16)

    @pl.when(step == pl.num_programs(0) - 1)
    def _():
        fetch.wait()
        every = jnp.concatenate([hidden[one] for one in range(hidden.shape[0])], axis=1)
        for mask in range(count):
            columns = pl.ds(pl.multiple_of((me_y ^ mask) * width, width), width)
            terms = jnp.dot(every, held[:, columns], preferred_element_type=F32).astype(BF16)
            for block in range(blocks):
                (odd if mask % 2 else even)[mask // 2, block] = terms[
                    block * rows : (block + 1) * rows, :
                ]


def per_device(
    tokens,
    attention_gain,
    projection_weight,
    output_weight,
    prompt_cache,
    cache_length,
    prompt_group,
    parents,
    accepted_path,
    expert_gain,
    gate_up_weight,
    down_weight,
    route_experts,
    route_gates,
):
    gx_count, gy_count = lax.axis_size("gx"), lax.axis_size("gy")
    ids = jnp.stack([lax.axis_index("gx"), lax.axis_index("gy")]).astype(jnp.int32)
    rows, width = tokens.shape
    depth = attention_gain.shape[0]
    requests, draft = parents.shape
    groups = prompt_cache.shape[0]
    heads = width // HD

    wide_tokens = tokens.astype(F32)
    squares = jnp.sum(wide_tokens * wide_tokens, axis=1, keepdims=True)
    for bit in range(gy_count.bit_length() - 1):
        squares = squares + swap(squares, "gy", 1 << bit)
    row_scale = lax.rsqrt(squares / depth + 1e-05)

    weight = jnp.transpose(projection_weight, (1, 0, 2))
    share = gy_count // gx_count
    terms_of = gx_count // 2
    route = [
        (
            a * gy_count + b,
            (b // share // 2 * 2 + a % 2) * gy_count
            + (a // 2 * 2 + b // share % 2) * share
            + b % share,
        )
        for a in range(gx_count)
        for b in range(gy_count)
    ]
    moved = lax.ppermute(tokens, ("gx", "gy"), route)
    other_weight = swap(weight, "gx", 1)
    experts = gate_up_weight.shape[0]
    units = gate_up_weight.shape[3]
    output_weight, moved = lax.optimization_barrier((output_weight, moved))
    near_output = [output_weight] + [
        swap(output_weight, "gx", 2 * far) for far in range(1, terms_of)
    ]
    far = gather_far(moved)
    gate_up, far, near_output = lax.optimization_barrier(
        (jnp.transpose(gate_up_weight, (2, 0, 1, 3)), far, near_output)
    )
    pieces = gather_near(far)
    types = [F32] + [BF16] * (terms_of - 1)
    projected = pl.pallas_call(
        lambda *refs: project_kernel(gy_count, share, *refs),
        out_shape=[jax.ShapeDtypeStruct((rows, width), kind) for kind in types]
        + [jax.ShapeDtypeStruct((2, rows, width), kind) for kind in types],
        in_specs=[smem()] + [vmem()] * (3 + gy_count),
        out_specs=[vmem()] * (2 * terms_of),
        scratch_shapes=[pltpu.VMEM((2, terms_of * rows, share * width), BF16)],
        compiler_params=params(),
        name="project",
    )(ids, attention_gain.reshape(1, depth), weight, other_weight, *pieces)
    query_terms, pair_terms = projected[:terms_of], projected[terms_of:]
    parents, query_terms = lax.optimization_barrier((parents, query_terms))
    query_terms = [query_terms[0]] + [
        swap(query_terms[far], "gx", 2 * far) for far in range(1, terms_of)
    ]
    pair_terms, near_output, query_terms = lax.optimization_barrier(
        (list(pair_terms), near_output, query_terms)
    )
    pair_terms = [pair_terms[0]] + [
        swap(pair_terms[far], "gx", 2 * far) for far in range(1, terms_of)
    ]
    output_blocks = [one for held in near_output for one in (held, swap(held, "gx", 1))]

    owner = prompt_group % groups
    order = jnp.arange(requests, dtype=jnp.int32)
    ahead = (owner[None, :] < owner[:, None]) | (
        (owner[None, :] == owner[:, None]) & (order[None, :] < order[:, None])
    )
    place = jnp.sum(ahead.astype(jnp.int32), axis=1)
    group_ids = jnp.arange(groups, dtype=jnp.int32)
    held = jnp.sum((owner[None, :] == group_ids[:, None]).astype(jnp.int32), axis=1)
    first = jnp.sum((owner[None, :] < group_ids[:, None]).astype(jnp.int32), axis=1)

    slots = prompt_cache.shape[2]
    step = min(CACHE_BLOCK, slots)
    wide_rows = heads * draft
    flat = lambda *_: (0, 0)
    top, mass, mixed, query = pl.pallas_call(
        lambda *refs: cache_kernel(requests, draft, heads, terms_of, *refs),
        grid_spec=pltpu.PrefetchScalarGridSpec(
            num_scalar_prefetch=4,
            grid=(groups, slots // step),
            in_specs=[pl.BlockSpec((rows, 1), flat)]
            + [pl.BlockSpec((rows, width), flat)] * terms_of
            + [
                pl.BlockSpec(
                    (1, 2, step, width),
                    lambda group, block, lengths, first, held, place: (
                        group,
                        0,
                        jnp.where(
                            held[group] > 0, jnp.minimum(block, (lengths[group] - 1) // step), 0
                        ),
                        0,
                    ),
                ),
            ],
            out_specs=[
                pl.BlockSpec((requests * wide_rows, HD), flat),
                pl.BlockSpec((requests * wide_rows, HD), flat),
                pl.BlockSpec((requests * wide_rows, width), flat),
                pl.BlockSpec((rows, width), flat),
            ],
            scratch_shapes=[pltpu.VMEM((requests * wide_rows, width), BF16)],
        ),
        out_shape=(
            jax.ShapeDtypeStruct((requests * wide_rows, HD), F32),
            jax.ShapeDtypeStruct((requests * wide_rows, HD), F32),
            jax.ShapeDtypeStruct((requests * wide_rows, width), F32),
            jax.ShapeDtypeStruct((rows, width), BF16),
        ),
        compiler_params=params(),
        cost_estimate=cost(20 * rows * slots * width, 4 * groups * slots * width),
        name="cache",
    )(cache_length, first, held, place, row_scale, *query_terms, prompt_cache)

    accepted = accepted_path.shape[1]
    chosen = (jnp.arange(requests, dtype=jnp.int32)[:, None] * draft + accepted_path).reshape(-1, 1)
    half = jax.ShapeDtypeStruct((gy_count // 2, rows, width), BF16)
    even, odd, picked = pl.pallas_call(
        lambda *refs: draft_kernel(requests, draft, heads, terms_of, gy_count, *refs),
        out_shape=(
            half,
            half,
            jax.ShapeDtypeStruct((2, requests * accepted, width), BF16),
        ),
        in_specs=[smem(), smem()] + [vmem()] * (terms_of + 7 + gx_count),
        out_specs=(vmem(), vmem(), vmem()),
        scratch_shapes=[pltpu.VMEM((rows, width), BF16)] * 3 + [pltpu.VMEM((depth, width), BF16)],
        compiler_params=params(),
        name="draft",
    )(
        ids,
        place,
        row_scale,
        *pair_terms,
        query,
        ancestor_table(parents),
        chosen,
        top,
        mass,
        mixed,
        *output_blocks,
    )
    compacted = jnp.transpose(picked, (1, 0, 2))

    summed = even.astype(F32) + swap(odd, "gy", 1).astype(F32)
    stream = tokens.astype(F32) + summed[0]
    for place in range(1, gy_count // 2):
        stream = stream + swap(summed[place].astype(BF16), "gy", 2 * place).astype(F32)
    stream = stream.astype(BF16)

    units_of = [(one, one + 2) for one in range(gx_count) if not one & 2]
    blocks = {0: stream, units_of[0][1]: swap(stream, "gx", units_of[0][1])}
    later, blocks[units_of[0][1]] = lax.optimization_barrier((stream, blocks[units_of[0][1]]))
    for mask in range(gx_count):
        if mask not in blocks:
            blocks[mask] = swap(later, "gx", mask)
    inputs = [one for mask in units_of[0] for one in gather_gy(blocks[mask])]
    result = stream.astype(F32)
    waiting, last = [], None
    half = jax.ShapeDtypeStruct((gy_count // 2, 2, rows, width), BF16)
    for number, masks in enumerate(units_of):
        after = []
        if number + 1 < len(units_of):
            after = [jnp.stack([blocks[mask] for mask in units_of[number + 1]])]
        inputs, waiting, after = lax.optimization_barrier((inputs, waiting, after))
        far = [gather_far(one) for one in after]
        arrived = [swap(one, "gy", 2 * place) for place, one in enumerate(waiting) if place]
        odd, even = pl.pallas_call(
            lambda *refs: expert_kernel(gy_count, masks, number > 0, *refs),
            grid=(experts,),
            in_specs=[
                smem(),
                pl.BlockSpec((1, depth), lambda expert: (0, 0)),
                vmem(),
                vmem(),
                pl.BlockSpec((2, 1, depth, units), lambda expert: (0, expert, 0, 0)),
                pl.BlockSpec(memory_space=pl.ANY),
            ]
            + [vmem()] * len(inputs),
            out_specs=[vmem(), vmem()],
            out_shape=(half, half),
            scratch_shapes=[
                pltpu.VMEM((2 * rows, depth), BF16),
                pltpu.VMEM((experts, 2 * rows, units), BF16),
                pltpu.VMEM((experts * units, depth), BF16),
                pltpu.SemaphoreType.DMA,
            ],
            compiler_params=params(),
            cost_estimate=cost(12 * rows * depth * experts * units, 6 * depth * experts * units),
            name="experts",
        )(
            ids,
            expert_gain.reshape(1, depth),
            route_experts.T,
            route_gates.astype(F32).T,
            gate_up,
            down_weight.reshape(experts * units, depth),
            *inputs,
        )
        odd, even, far, arrived = lax.optimization_barrier((odd, even, far, arrived))
        if waiting:
            total = sum([one.astype(F32) for one in arrived], waiting[0])
            for mask, one in zip(last, total):
                if mask:
                    one = swap(one.astype(BF16), "gx", mask).astype(F32)
                result = result + one
        last = masks
        near = swap(odd, "gy", 1)
        inputs = [one for pieces in far for one in gather_near(pieces)]
        summed = even.astype(F32) + near.astype(F32)
        if after:
            waiting = [summed[0]] + [one.astype(BF16) for one in summed[1:]]
        else:
            totals, result = halve_gy([summed[:, turn] for turn in range(len(masks))], result)
    for mask, one in zip(masks, totals):
        if mask:
            one = swap(one.astype(BF16), "gx", mask).astype(F32)
        result = result + one
    return (result.astype(BF16), compacted)


def gather_far(value):
    return [value] + [swap(value, "gy", mask) for mask in range(2, lax.axis_size("gy"), 2)]


def gather_near(even):
    return [one for held in even for one in (held, swap(held, "gy", 1))]


def gather_gy(value):
    return gather_near(gather_far(value))


def far_bits(turn):
    bits = list(range(1, lax.axis_size("gy").bit_length() - 1))
    return bits[::-1] if turn else bits


def halve_gy(values, early):
    many = [[(2 * place, value[place]) for place in range(value.shape[0])] for value in values]
    orders = [far_bits(turn % 2) for turn in range(len(values))]
    for step in range(len(orders[0])):
        sent = [
            jnp.stack([one for mask, one in held if mask >> order[step] & 1]).astype(BF16)
            for held, order in zip(many, orders)
        ]
        if step + 1 == len(orders[0]):
            sent, early = lax.optimization_barrier((sent, early))
        for turn, order in enumerate(orders):
            got = swap(sent[turn], "gy", 1 << order[step]).astype(F32)
            mine = [(mask, one) for mask, one in many[turn] if not mask >> order[step] & 1]
            many[turn] = [(mask, one + got[place]) for place, (mask, one) in enumerate(mine)]
    return [held[0][1] for held in many], early


def solution(mesh):
    placed = (
        P("gx", "gy"),
        P(),
        P("gx", None, "gy"),
        P("gx", "gy"),
        P("gx", None, None, "gy"),
        P("gx"),
        P("gx"),
        P("gx", None),
        P("gx", None),
        P(),
        P("gy", None, None, "gx"),
        P("gy", "gx", None),
        P(),
        P(),
    )
    return jax.shard_map(
        per_device,
        mesh=mesh,
        in_specs=placed,
        out_specs=(P("gx", "gy"), P("gx", None, "gy")),
        check_vma=False,
    )
```
